32 devices in a mesh: row: 8 (over z, core), col: 4 (over y, x).
Axes of the slice: x: 2, y: 2, z: 4, core: 2. Of those that a mesh axis runs over, the one named last changes fastest.
Arguments:
- tokens: bfloat16 [2048, 8192], P('row', 'col'), may hold values from -6 to 6
- out_grad: bfloat16 [2048, 8192], P('row', 'col'), may hold values from -1.5 to 1.5
- gate_weight: bfloat16 [112, 1024, 128], P('col', 'row'), may hold values from -0.1875 to 0.1875
- up_weight: bfloat16 [112, 1024, 128], P('col', 'row'), may hold values from -0.1875 to 0.1875
- down_weight: bfloat16 [112, 1024, 128], P('col', 'row'), may hold values from -0.125 to 0.125
- gate_rows: int32 [112, 8], P('col'), may hold values from 0 to 63, all different within a row
- up_rows: int32 [112, 8], P('col'), may hold values from 0 to 63, all different within a row
- down_columns: int32 [112, 8], P('col'), may hold values from 0 to 63, all different within a row
Outputs:
- output: bfloat16 [2048, 8192], P('row', 'col')
- input_grad: bfloat16 [2048, 8192], P('row', 'col')
- gate_weight_grad: bfloat16 [112, 1024, 128], P('col', 'row')
- up_weight_grad: bfloat16 [112, 1024, 128], P('col', 'row')
- down_weight_grad: bfloat16 [112, 1024, 128], P('col', 'row')
The draws below stay inside these ranges and needn't reach their ends.
Inputs may be any that keep to these rules, and one draw needn't show every extreme that they name: `gate_rows`: each row names 8 different block-rows; every block-row is named in some row. `up_rows`: each row names 8 different block-rows; every block-row is named in some row. `down_columns`: each row names 8 different output block-columns; every block-column is named in some row.
All inputs are finite; a program needn't handle non-finite values.
Results may differ from the reference program's by a relative error of at most 0.018.
Values may be sent and summed in bfloat16 or wider, within the bound.
No kernel may reach another device: no remote copies, remote signals or barrier semaphores. Data moves between devices by JAX's collectives and lax.ppermute only.
A program may use at most 192 MiB of HBM per device.

```python
import jax
import jax.numpy as jnp
from jax import lax

D = 8192
BS = 128
KG = 8
KH = 8
TOK_ROW = 256
DB = 64
FB = 112
FBC = 28
TOKENS = 2048
N_ROW = 8
N_COL = 4


def shard_levels(key, extent, shards, low, high):
    factor_of = 1.0
    for dim, shards_of in shards:
        steps = jax.random.uniform(jax.random.fold_in(jax.random.fold_in(key, 6), dim), (shards_of,), jnp.float32, low / len(shards), high / len(shards))
        factor_of = factor_of * jnp.repeat(jnp.exp(steps), extent[dim] // shards_of).reshape((-1,) + (1,) * (len(extent) - 1 - dim))
    return factor_of


def distinct(key, rows, number_of, top, lift):
    ranking = jax.random.permutation(jax.random.fold_in(key, 1), number_of)
    boost = ranking
    for power in range(3):
        boost = boost * boost // number_of
    boost = boost * lift // number_of
    chance = jax.random.randint(jax.random.fold_in(key, 2), (rows, number_of), 0, 4096) + boost
    fixed_rows = jax.random.permutation(jax.random.fold_in(key, 3), rows)[jnp.arange(number_of) % rows]
    chance = jnp.where(jnp.arange(rows)[:, None] == fixed_rows[None, :], 1 << 14, chance)
    score = chance * number_of + jnp.arange(number_of)
    return lax.top_k(score.astype(jnp.int32), top)[1].astype(jnp.int32)


def noise(stream_key, shape, deviation, limit, pieces=(), held_as=jnp.bfloat16):
    loudness = shard_levels(stream_key, shape, pieces, -0.22, 0.18) if pieces else 1.0
    array = jax.random.normal(stream_key, shape, jnp.float32) * deviation * loudness
    return jnp.minimum(jnp.maximum(array, -limit), limit).astype(held_as)


def setup_inputs(seed: int = 0) -> dict:
    keys = jax.random.split(jax.random.key(seed), 9)
    return {
        "tokens": noise(keys[0], (TOKENS, D), 1.0, 6.0, ((0, 8), (1, 4))),
        "out_grad": noise(keys[1], (TOKENS, D), 0.25, 1.5, ((0, 8), (1, 4))),
        "gate_weight": noise(keys[2], (FB, KG * BS, BS), (KG * BS) ** -0.5, 0.1875, ((0, 4), (1, 8))),
        "up_weight": noise(keys[3], (FB, KG * BS, BS), (KG * BS) ** -0.5, 0.1875, ((0, 4), (1, 8))),
        "down_weight": noise(keys[4], (FB, KH * BS, BS), (FB * KH * BS // DB) ** -0.5, 0.125, ((0, 4), (1, 8))),
        "gate_rows": distinct(keys[5], FB, DB, KG, 0),
        "up_rows": distinct(keys[6], FB, DB, KG, 1024),
        "down_columns": distinct(keys[7], FB, DB, KH, 2048),
    }


def rounded(values):
    return lax.optimization_barrier(values.astype(jnp.bfloat16)).astype(jnp.float32)


def spread(contrib, block_lists):
    zero_block = jnp.zeros((TOKENS, DB, BS), jnp.float32)
    return zero_block.at[:, block_lists.reshape(-1)].add(contrib.reshape(TOKENS, -1, BS))


def by_group(values):
    return values.reshape((N_ROW, TOK_ROW) + values.shape[1:])


def group_sum(partial_value):
    return jnp.sum(rounded(partial_value), axis=0).astype(jnp.bfloat16)


def reference(tokens, out_grad, gate_weight, up_weight, down_weight, gate_rows, up_rows, down_columns):
    highest = lax.Precision.HIGHEST
    blocks_in = tokens.astype(jnp.float32).reshape(TOKENS, DB, BS)
    blocks_grad = out_grad.astype(jnp.float32).reshape(TOKENS, DB, BS)

    def column(totals, column_index):
        out_total, in_total = totals
        first_slot = column_index * FBC
        gate_tiles = lax.dynamic_slice_in_dim(gate_weight, first_slot, FBC, 0).astype(jnp.float32).reshape(FBC, KG, BS, BS)
        up_tiles = lax.dynamic_slice_in_dim(up_weight, first_slot, FBC, 0).astype(jnp.float32).reshape(FBC, KG, BS, BS)
        down_tiles = lax.dynamic_slice_in_dim(down_weight, first_slot, FBC, 0).astype(jnp.float32).reshape(FBC, KH, BS, BS)
        gate_list = lax.dynamic_slice_in_dim(gate_rows, first_slot, FBC, 0)
        up_list = lax.dynamic_slice_in_dim(up_rows, first_slot, FBC, 0)
        down_list = lax.dynamic_slice_in_dim(down_columns, first_slot, FBC, 0)
        picked_gate = jnp.take(blocks_in, gate_list.reshape(-1), axis=1).reshape(TOKENS, FBC, KG, BS)
        picked_up = jnp.take(blocks_in, up_list.reshape(-1), axis=1).reshape(TOKENS, FBC, KG, BS)
        picked_grad = jnp.take(blocks_grad, down_list.reshape(-1), axis=1).reshape(TOKENS, FBC, KH, BS)
        gate_value = jnp.einsum('tfkr,fkri->tfi', picked_gate, gate_tiles, precision=highest)
        up_value = jnp.einsum('tfkr,fkri->tfi', picked_up, up_tiles, precision=highest)
        sigmoid_gate = jax.nn.sigmoid(gate_value)
        silu_gate = gate_value * sigmoid_gate
        hidden = rounded(silu_gate * up_value)
        out_part = jnp.einsum('tfi,fkji->tfkj', hidden, down_tiles, precision=highest)
        out_total = out_total + rounded(spread(out_part, down_list))
        hidden_grad = jnp.einsum('tfkj,fkji->tfi', picked_grad, down_tiles, precision=highest)
        gate_grad = rounded(hidden_grad * up_value * sigmoid_gate * (1.0 + gate_value * (1.0 - sigmoid_gate)))
        up_grad = rounded(hidden_grad * silu_gate)
        from_gate = jnp.einsum('tfi,fkri->tfkr', gate_grad, gate_tiles, precision=highest)
        from_up = jnp.einsum('tfi,fkri->tfkr', up_grad, up_tiles, precision=highest)
        in_total = in_total + rounded(spread(from_gate, gate_list) + spread(from_up, up_list))
        gate_tile_grad = group_sum(jnp.einsum('ntfkr,ntfi->nfkri', by_group(picked_gate), by_group(gate_grad), precision=highest))
        up_tile_grad = group_sum(jnp.einsum('ntfkr,ntfi->nfkri', by_group(picked_up), by_group(up_grad), precision=highest))
        down_tile_grad = group_sum(jnp.einsum('ntfkj,ntfi->nfkji', by_group(picked_grad), by_group(hidden), precision=highest))
        return (out_total, in_total), (gate_tile_grad, up_tile_grad, down_tile_grad)

    initial = (jnp.zeros((TOKENS, DB, BS), jnp.float32), jnp.zeros((TOKENS, DB, BS), jnp.float32))
    totals, tile_grads = lax.scan(column, initial, jnp.arange(N_COL, dtype=jnp.int32))
    output = totals[0].reshape(TOKENS, D).astype(jnp.bfloat16)
    input_grad = totals[1].reshape(TOKENS, D).astype(jnp.bfloat16)
    return (output, input_grad, tile_grads[0].reshape(FB, KG * BS, BS), tile_grads[1].reshape(FB, KG * BS, BS), tile_grads[2].reshape(FB, KH * BS, BS))
```

```python
import functools

import jax
import jax.numpy as jnp
from jax import lax
from jax.experimental import pallas as pl
from jax.experimental.pallas import tpu as pltpu
from jax.sharding import PartitionSpec as P

BS = 128
BF = jnp.bfloat16
F32 = jnp.float32


def contract(a, b, da, db):
    return lax.dot_general(a, b, (((da,), (db,)), ((), ())), preferred_element_type=F32)


def chunk_kernel(scal, *refs, n_col, slots, kg, f_total, f_first, blocks, first, last):
    refs = list(refs)

    def take(count):
        got = refs[:count]
        del refs[:count]
        return got

    x_hbm, y_hbm = take(n_col), take(n_col)
    acc_in = [] if first else take(2)
    tiles = take(slots)
    tile_grads = take(slots)
    results = take(2 * n_col) if last else take(2)
    x_all, y_all, acc_out, acc_x, load_sem, acc_sem, store_sem = refs

    step = pl.program_id(0)
    steps = pl.num_programs(0)
    tokens = x_all.shape[1]
    order = 3 * f_total * kg
    me = scal[order + kg]

    x_loads = [pltpu.make_async_copy(x_hbm[s], x_all.at[s], load_sem.at[0, s]) for s in range(n_col)]
    y_loads = [pltpu.make_async_copy(y_hbm[s], y_all.at[s], load_sem.at[1, s]) for s in range(n_col)]
    totals = (acc_out, acc_x)
    acc_loads = [pltpu.make_async_copy(src, dst, acc_sem.at[i]) for i, (src, dst) in enumerate(zip(acc_in, totals))]

    @pl.when(step == 0)
    def _():
        for copy in x_loads + y_loads + acc_loads:
            copy.start()
        if first:
            for total in totals:
                total[...] = jnp.zeros_like(total)
        for copy in x_loads:
            copy.wait()

    def places(table):
        found = []
        for s in range(kg):
            block = scal[table * f_total * kg + (f_first + step) * kg + scal[order + s]]
            slot = (block // blocks) ^ me
            found.append((slot, pl.multiple_of(lax.rem(block, blocks) * BS, BS)))
        return found

    def picked(source, where):
        return jnp.concatenate([source[slot, :, pl.ds(at, BS)] for slot, at in where], axis=1)

    def stacked(kind):
        return jnp.concatenate([tile[kind, 0] for tile in tiles], axis=0)

    def put(kind, grads):
        for s, ref in enumerate(tile_grads):
            ref[kind, 0] = grads[s * BS : (s + 1) * BS].astype(BF)

    def scatter(total, where, left, right):
        for s in range(0, kg, 2):
            two = contract(left, right[s * BS : (s + 2) * BS], 1, 1)
            for i in range(2):
                slot, at = where[s + i]
                total[slot, :, pl.ds(at, BS)] += two[:, i * BS : (i + 1) * BS]

    gate_at, up_at, down_at = places(0), places(1), places(2)
    gate_w, up_w, down_w = stacked(0), stacked(1), stacked(2)
    x_gate, x_up = picked(x_all, gate_at), picked(x_all, up_at)
    gate = contract(x_gate, gate_w, 1, 0)
    up = contract(x_up, up_w, 1, 0)
    sig = jax.nn.sigmoid(gate)
    silu = gate * sig
    hidden = (silu * up).astype(BF)

    @pl.when(step == 0)
    def _():
        for copy in y_loads:
            copy.wait()

    y_down = picked(y_all, down_at)
    hidden_grad = contract(y_down, down_w, 1, 0)
    gate_grad = (hidden_grad * up * sig * (1.0 + gate * (1.0 - sig))).astype(BF)
    up_grad = (hidden_grad * silu).astype(BF)
    put(2, contract(y_down, hidden, 0, 0))
    put(0, contract(x_gate, gate_grad, 0, 0))
    put(1, contract(x_up, up_grad, 0, 0))

    @pl.when(step == 0)
    def _():
        for copy in acc_loads:
            copy.wait()

    scatter(acc_out, down_at, hidden, down_w)
    scatter(acc_x, gate_at, gate_grad, gate_w)
    scatter(acc_x, up_at, up_grad, up_w)

    @pl.when(step == steps - 1)
    def _():
        if not last:
            stores = [pltpu.make_async_copy(src, dst, acc_sem.at[i]) for i, (src, dst) in enumerate(zip(totals, results))]
            for copy in stores:
                copy.start()
        else:
            stores = []
            for i, (total, rounded) in enumerate(zip(totals, (x_all, y_all))):
                for s in range(n_col):
                    for t in range(0, tokens, 32):
                        rounded[s, t : t + 32] = total[s, t : t + 32].astype(BF)
                    copy = pltpu.make_async_copy(rounded.at[s], results[i * n_col + s], store_sem.at[i, s])
                    copy.start()
                    stores.append(copy)
        for copy in stores:
            copy.wait()


def run_chunk(scal, xs, ys, accs, tiles, *, f_total, f_first, last):
    n_col, slots = len(xs), len(tiles)
    tokens, width = xs[0].shape
    f_here = tiles[0].shape[1]
    kg = slots
    first = accs is None
    anywhere = pl.BlockSpec(memory_space=pl.ANY)
    tile_spec = pl.BlockSpec((3, 1, BS, BS), lambda f, scal: (0, f, 0, 0))
    tile_shape = jax.ShapeDtypeStruct((3, f_here, BS, BS), BF)
    acc_shape = jax.ShapeDtypeStruct((n_col, tokens, width), F32)
    slice_shape = jax.ShapeDtypeStruct((tokens, width), BF)
    results = [slice_shape] * (2 * n_col) if last else [acc_shape] * 2
    kernel = functools.partial(
        chunk_kernel,
        n_col=n_col,
        slots=slots,
        kg=kg,
        f_total=f_total,
        f_first=f_first,
        blocks=width // BS,
        first=first,
        last=last,
    )
    flops = 9 * 2 * tokens * f_here * kg * BS * BS
    out = pl.pallas_call(
        kernel,
        grid_spec=pltpu.PrefetchScalarGridSpec(
            num_scalar_prefetch=1,
            grid=(f_here,),
            in_specs=[anywhere] * (2 * n_col + (0 if first else 2)) + [tile_spec] * slots,
            out_specs=[tile_spec] * slots + [anywhere] * len(results),
            scratch_shapes=[
                pltpu.VMEM((n_col, tokens, width), BF),
                pltpu.VMEM((n_col, tokens, width), BF),
                pltpu.VMEM((n_col, tokens, width), F32),
                pltpu.VMEM((n_col, tokens, width), F32),
                pltpu.SemaphoreType.DMA((2, n_col)),
                pltpu.SemaphoreType.DMA((2,)),
                pltpu.SemaphoreType.DMA((2, n_col)),
            ],
        ),
        out_shape=[tile_shape] * slots + results,
        compiler_params=pltpu.CompilerParams(vmem_limit_bytes=48 * 1024 * 1024),
        cost_estimate=pl.CostEstimate(flops=flops, bytes_accessed=40 * 1024 * 1024, transcendentals=0),
        name="ffn_chunk",
    )(scal, *xs, *ys, *([] if first else accs), *tiles)
    return out[:slots], out[slots:]


def total_of(*terms):
    value = terms[0].astype(F32)
    for term in terms[1:]:
        value = value + term.astype(F32)
    return value.astype(BF)


def make_shards(n_row, n_col):
    nz = n_row // 2

    def right(first, stop):
        return [(2 * z + c, 2 * z + 2 + c) for z in range(first, stop) for c in (0, 1)]

    def left(first, stop):
        return [(2 * z + c, 2 * z - 2 + c) for z in range(first, stop) for c in (0, 1)]

    across = [(r, r ^ 1) for r in range(n_row)]

    def from_columns(piece):
        return [piece] + [lax.ppermute(piece, "col", [(i, i ^ o) for i in range(n_col)]) for o in range(1, n_col)]

    def gather_chain(own, after):
        z = lax.axis_index("row") // 2
        own, _ = lax.optimization_barrier((own, after))
        rights, lefts = [own], [own]
        for s in range(1, nz):
            rights.append(lax.ppermute(rights[-1], "row", right(s - 1, nz - 1)))
            lefts.append(lax.ppermute(lefts[-1], "row", left(1, nz - s + 1)))
        slots = [own] + [jnp.where(z >= o, rights[o], lefts[nz - o]) for o in range(1, nz)]
        marker = (rights[min(2, nz - 1)], lefts[min(2, nz - 1)])
        return slots, marker

    def reduce_chain(own, sent):
        got = [lax.ppermute(part, "row", across) for part in sent]
        from_left = from_right = ()
        for s in range(1, nz):
            to_right = total_of(own[s], got[s], *from_left)
            to_left = total_of(own[nz - s], got[nz - s], *from_right)
            from_left = (lax.ppermute(to_right, "row", right(0, s)),)
            from_right = (lax.ppermute(to_left, "row", left(nz - s, nz)),)
        return total_of(own[0], got[0], *from_left, *from_right)

    def sum_columns(parts):
        return total_of(*[parts[0]] + [lax.ppermute(parts[o], "col", [(i, i ^ o) for i in range(n_col)]) for o in range(1, n_col)])

    def shards(tokens, out_grad, gate_weight, up_weight, down_weight, gate_rows, up_rows, down_columns):
        f_total, part = gate_weight.shape[:2]
        kg = gate_rows.shape[1]
        row = lax.axis_index("row")
        z, core = row // 2, row % 2
        whole_tiles = part == BS
        spots = (z - jnp.arange(nz, dtype=jnp.int32)) % nz
        order = jnp.concatenate([2 * spots + core, 2 * spots + 1 - core]) if whole_tiles else spots
        scal = jnp.concatenate(
            [t.reshape(-1) for t in (gate_rows, up_rows, down_columns)]
            + [order.astype(jnp.int32), lax.axis_index("col").astype(jnp.int32).reshape(1)]
        )
        xs, ys = from_columns(tokens), from_columns(out_grad)

        pieces = 4 if f_total % 4 == 0 else 1
        size = f_total // pieces
        after = ()
        accs, grads = None, []
        for piece in range(pieces):
            f_first = piece * size
            own = jnp.stack([w[f_first : f_first + size] for w in (gate_weight, up_weight, down_weight)])
            mine, after = gather_chain(own, after)
            other = [lax.ppermute(m, "row", across) for m in mine]
            if whole_tiles:
                tiles = mine + other
            else:
                tiles = [
                    jnp.where(core == 0, jnp.concatenate([a, b], 2), jnp.concatenate([b, a], 2))
                    for a, b in zip(mine, other)
                ]
            tile_grads, accs = run_chunk(
                scal, xs, ys, accs, tiles, f_total=f_total, f_first=f_first, last=piece == pieces - 1
            )
            if whole_tiles:
                keep, give = tile_grads[:nz], tile_grads[nz:]
            else:
                keep = [lax.dynamic_slice_in_dim(g, core * part, part, 2) for g in tile_grads]
                give = [lax.dynamic_slice_in_dim(g, (1 - core) * part, part, 2) for g in tile_grads]
            grads.append(reduce_chain(keep, give))

        output, input_grad = sum_columns(accs[:n_col]), sum_columns(accs[n_col:])
        weight_grads = [jnp.concatenate([g[kind] for g in grads], axis=0) for kind in range(3)]
        return (output, input_grad, *weight_grads)

    return shards


def solution(mesh):
    in_specs = (
        P("row", "col"),
        P("row", "col"),
        P("col", "row", None),
        P("col", "row", None),
        P("col", "row", None),
        P("col", None),
        P("col", None),
        P("col", None),
    )
    out_specs = in_specs[:5]
    shards = make_shards(mesh.shape["row"], mesh.shape["col"])
    return jax.shard_map(shards, mesh=mesh, in_specs=in_specs, out_specs=out_specs, check_vma=False)
```

```python
import functools

import jax
import jax.numpy as jnp
from jax import lax
from jax.experimental import pallas as pl
from jax.experimental.pallas import tpu as pltpu
from jax.sharding import PartitionSpec as P

BS = 128
BF = jnp.bfloat16
F32 = jnp.float32


def contract(a, b, da, db):
    return lax.dot_general(a, b, (((da,), (db,)), ((), ())), preferred_element_type=F32)


def chunk_kernel(scal, *refs, n_col, pieces, groups, waits, kg, f_total, f_first, blocks, first, last):
    refs = list(refs)

    def take(count):
        got = refs[:count]
        del refs[:count]
        return got

    (panels,) = take(1)
    take(waits)
    acc_in = [] if first else take(2)
    tiles = take(groups)
    tile_grads = take(groups)
    results = take(len(pieces)) if last else take(2)
    x_all, y_all, acc_out, acc_x, load_sem, acc_sem, store_sem = refs

    step = pl.program_id(0)
    steps = pl.num_programs(0)
    tokens = x_all.shape[1]
    order = 3 * f_total * kg
    me = scal[order + kg]
    both = (x_all, y_all)
    totals = (acc_out, acc_x)

    x_loads, y_loads = [
        [pltpu.make_async_copy(panels.at[slot, kind], both[kind].at[slot], load_sem.at[kind, slot]) for slot in range(n_col)]
        for kind in range(2)
    ]
    acc_loads = [pltpu.make_async_copy(src, dst, acc_sem.at[i]) for i, (src, dst) in enumerate(zip(acc_in, totals))]

    @pl.when(step == 0)
    def _():
        for copy in x_loads + y_loads + acc_loads:
            copy.start()
        if first:
            for total in totals:
                total[...] = jnp.zeros_like(total)
        for copy in x_loads:
            copy.wait()

    def places(table):
        found = []
        for s in range(kg):
            block = scal[table * f_total * kg + (f_first + step) * kg + scal[order + s]]
            found.append((block // blocks, pl.multiple_of(lax.rem(block, blocks) * BS, BS)))
        return found

    def picked(source, where):
        return jnp.concatenate([source[slot, :, pl.ds(at, BS)] for slot, at in where], axis=1)

    def stacked(kind):
        return jnp.concatenate([tile[i, kind, 0] for tile in tiles for i in range(tile.shape[0])], axis=0)

    def put(kind, grads):
        s = 0
        for ref in tile_grads:
            for i in range(ref.shape[0]):
                ref[i, kind, 0] = grads[:, s * BS : (s + 1) * BS].astype(BF)
                s += 1

    def scatter(total, where, left, right):
        for s in range(0, kg, 2):
            two = contract(left, right[s * BS : (s + 2) * BS], 1, 1)
            for i in range(2):
                slot, at = where[s + i]
                total[slot ^ me, :, pl.ds(at, BS)] += two[:, i * BS : (i + 1) * BS]

    gate_at, up_at, down_at = places(0), places(1), places(2)
    gate_w, up_w, down_w = stacked(0), stacked(1), stacked(2)
    x_gate, x_up = picked(x_all, gate_at), picked(x_all, up_at)
    gate = contract(x_gate, gate_w, 1, 0)
    up = contract(x_up, up_w, 1, 0)
    sig = jax.nn.sigmoid(gate)
    silu = gate * sig
    hidden = (silu * up).astype(BF)

    @pl.when(step == 0)
    def _():
        for copy in y_loads:
            copy.wait()

    y_down = picked(y_all, down_at)
    hidden_grad = contract(y_down, down_w, 1, 0)
    gate_grad = (hidden_grad * up * sig * (1.0 + gate * (1.0 - sig))).astype(BF)
    up_grad = (hidden_grad * silu).astype(BF)
    put(2, contract(hidden, y_down, 0, 0))
    put(0, contract(gate_grad, x_gate, 0, 0))
    put(1, contract(up_grad, x_up, 0, 0))

    @pl.when(step == 0)
    def _():
        for copy in acc_loads:
            copy.wait()

    scatter(acc_out, down_at, hidden, down_w)
    scatter(acc_x, gate_at, gate_grad, gate_w)
    scatter(acc_x, up_at, up_grad, up_w)

    @pl.when(step == steps - 1)
    def _():
        stores = []
        for kind, (total, rounded) in enumerate(zip(totals, both)):
            if last:
                for s in range(n_col):
                    for t in range(0, tokens, 32):
                        rounded[s, t : t + 32] = total[s, t : t + 32].astype(BF)
                here = [
                    pltpu.make_async_copy(
                        rounded.at[slot, pl.ds(at, rows)], results[p].at[kind], store_sem.at[kind, p]
                    )
                    for p, (slot, at, rows) in enumerate(pieces)
                ]
            else:
                here = [pltpu.make_async_copy(total, results[kind], acc_sem.at[kind])]
            for copy in here:
                copy.start()
            stores += here
        for copy in stores:
            copy.wait()


def run_chunk(scal, panels, after, pieces, accs, tiles, *, f_total, f_first, f_here, tile_first, last):
    n_col, _, tokens, width = panels.shape
    kg = sum(t.shape[0] for t in tiles)
    first = accs is None
    anywhere = pl.BlockSpec(memory_space=pl.ANY)
    tile_specs = [pl.BlockSpec((t.shape[0], 3, 1, BS, BS), lambda f, scal: (0, 0, f + tile_first, 0, 0)) for t in tiles]
    grad_specs = [pl.BlockSpec((t.shape[0], 3, 1, BS, BS), lambda f, scal: (0, 0, f, 0, 0)) for t in tiles]
    grad_shapes = [jax.ShapeDtypeStruct((t.shape[0], 3, f_here, BS, BS), BF) for t in tiles]
    if last:
        results = [jax.ShapeDtypeStruct((2, rows, width), BF) for _, _, rows in pieces]
    else:
        results = [jax.ShapeDtypeStruct((n_col, tokens, width), F32)] * 2
    kernel = functools.partial(
        chunk_kernel,
        n_col=n_col,
        pieces=pieces,
        groups=len(tiles),
        waits=len(after),
        kg=kg,
        f_total=f_total,
        f_first=f_first,
        blocks=width // BS,
        first=first,
        last=last,
    )
    flops = 9 * 2 * tokens * f_here * kg * BS * BS
    out = pl.pallas_call(
        kernel,
        grid_spec=pltpu.PrefetchScalarGridSpec(
            num_scalar_prefetch=1,
            grid=(f_here,),
            in_specs=[anywhere] * (1 + len(after) + (0 if first else 2)) + tile_specs,
            out_specs=grad_specs + [anywhere] * len(results),
            scratch_shapes=[
                pltpu.VMEM((n_col, tokens, width), BF),
                pltpu.VMEM((n_col, tokens, width), BF),
                pltpu.VMEM((n_col, tokens, width), F32),
                pltpu.VMEM((n_col, tokens, width), F32),
                pltpu.SemaphoreType.DMA((2, n_col)),
                pltpu.SemaphoreType.DMA((2,)),
                pltpu.SemaphoreType.DMA((2, len(pieces))),
            ],
        ),
        out_shape=grad_shapes + results,
        compiler_params=pltpu.CompilerParams(vmem_limit_bytes=48 * 1024 * 1024),
        cost_estimate=pl.CostEstimate(flops=flops, bytes_accessed=64 * 1024 * 1024, transcendentals=0),
        name="ffn_chunk",
    )(scal, panels, *after, *([] if first else accs), *tiles)
    return out[: len(tiles)], out[len(tiles) :]


def total_of(*terms):
    value = terms[0].astype(F32)
    for term in terms[1:]:
        value = value + term.astype(F32)
    return value.astype(BF)


def make_shards(n_row, n_col):
    nz = n_row // 2
    across = [(r, r ^ 1) for r in range(n_row)]
    two_phase = n_col == 4

    def right(first, stop):
        return [(2 * z + c, 2 * z + 2 + c) for z in range(first, stop) for c in (0, 1)]

    def left(first, stop):
        return [(2 * z + c, 2 * z - 2 + c) for z in range(first, stop) for c in (0, 1)]

    def over(value, offset):
        return lax.ppermute(value, "col", [(i, i ^ offset) for i in range(n_col)])

    def swap(value):
        return lax.ppermute(value, "row", across)

    def pieces_of(tokens):
        half = tokens // 2
        if two_phase:
            return ((0, 0, tokens), (1, 0, tokens), (2, 0, tokens), (3, 0, half), (3, half, half))
        return tuple((s, 0, tokens) for s in range(n_col))

    def sum_columns(parts):
        if two_phase:
            mine, beside, above, low, high = parts
            half = low.shape[1]
            low, high = over(low, 1), over(high, 2)
            above = jnp.concatenate([total_of(above[:, :half], low), above[:, half:]], axis=1)
            beside = jnp.concatenate([beside[:, :half], total_of(beside[:, half:], high)], axis=1)
            got = [over(beside, 1), over(above, 2)]
        else:
            mine = parts[0]
            got = [over(parts[o], o) for o in range(1, n_col)]
        return [total_of(mine[i], *[g[i] for g in got]) for i in range(2)]

    class Chain:
        def __init__(self, z, own=None, grads=None):
            self.z, self.own, self.grads = z, own, grads
            self.from_left, self.from_right = [], []
            self.tick = 0 if own is not None else 1

        def part(self, slot):
            return [g[slot // 2] for g in self.grads[slot % 2 :: 2]]

        def run(self, count):
            for _ in range(count):
                i = self.tick
                summing = self.grads is not None
                if i == 0:
                    to_right = to_left = self.own
                elif not summing:
                    to_right, to_left = self.from_left[-1], self.from_right[-1]
                else:
                    to_right = total_of(*self.part(i), *self.from_left[-1:])
                    to_left = total_of(*self.part(nz - i), *self.from_right[-1:])
                    if self.own is not None:
                        to_right = jnp.where(self.z >= i, self.from_left[-1], to_right)
                        to_left = jnp.where(nz - 1 - self.z >= i, self.from_right[-1], to_left)
                start = 0 if summing else i
                stop = nz - 1 if self.own is not None else i
                self.from_left.append(lax.ppermute(to_right, "row", right(start, stop)))
                self.from_right.append(lax.ppermute(to_left, "row", left(nz - stop, nz - start)))
                self.tick += 1
            return self

        def slots(self):
            found = [self.own]
            for o in range(1, nz):
                found.append(jnp.where(self.z >= o, self.from_left[o - 1], self.from_right[nz - o - 1]))
            return found

        def total(self):
            return total_of(*self.part(0), self.from_left[-1], self.from_right[-1])

    def shards(tokens, out_grad, gate_weight, up_weight, down_weight, gate_rows, up_rows, down_columns):
        f_total, part = gate_weight.shape[:2]
        kg = gate_rows.shape[1]
        row = lax.axis_index("row")
        z, core = row // 2, row % 2
        whole_tiles = part == BS
        slots = list(range(0, nz, 2)) + list(range(1, nz, 2))
        spots = (z - jnp.array(slots, dtype=jnp.int32)) % nz
        order = jnp.concatenate([2 * spots + core, 2 * spots + 1 - core]) if whole_tiles else spots
        scal = jnp.concatenate(
            [t.reshape(-1) for t in (gate_rows, up_rows, down_columns)]
            + [order.astype(jnp.int32), lax.axis_index("col").astype(jnp.int32).reshape(1)]
        )
        pieces = pieces_of(tokens.shape[0])
        panels = lax.all_gather(jnp.stack([tokens, out_grad]), "col")

        def own_tiles(start, stop):
            return jnp.stack([w[start:stop] for w in (gate_weight, up_weight, down_weight)])

        def all_tiles(mine):
            even, odd = jnp.stack(mine[0::2]), jnp.stack(mine[1::2])
            other_even, other_odd = swap(even), swap(odd)
            if whole_tiles:
                return [even, odd, other_even, other_odd]
            return [
                jnp.where(core == 0, jnp.concatenate([a, b], -2), jnp.concatenate([b, a], -2))
                for a, b in ((even, other_even), (odd, other_odd))
            ]

        def exchanged(tile_grads):
            if whole_tiles:
                keep, give = tile_grads[:2], tile_grads[2:]
            else:
                keep = [lax.dynamic_slice_in_dim(g, core * part, part, 4) for g in tile_grads]
                give = [lax.dynamic_slice_in_dim(g, (1 - core) * part, part, 4) for g in tile_grads]
            got_odd = swap(give[1])
            return [keep[0], keep[1], swap(give[0]), got_odd]

        if f_total % 4 == 0:
            sizes = [f_total // 4] * 4
        else:
            sizes = [f_total]
        starts = [sum(sizes[:i]) for i in range(len(sizes) + 1)]
        accs = None

        def compute(i, tiles, tile_first, accs, after=()):
            tile_grads, accs = run_chunk(
                scal,
                panels,
                after,
                pieces,
                accs,
                tiles,
                f_total=f_total,
                f_first=starts[i],
                f_here=sizes[i],
                tile_first=tile_first,
                last=i == len(sizes) - 1,
            )
            return exchanged(tile_grads), accs

        if len(sizes) == 1:
            gather = Chain(z, own_tiles(0, f_total)).run(nz - 1)
            grads, accs = compute(0, all_tiles(gather.slots()), 0, None)
            sums = [Chain(z, None, grads).run(nz - 1).total()]
        else:
            gather = Chain(z, own_tiles(0, starts[2])).run(nz - 1)
            tiles = all_tiles(gather.slots())
            one, two = Chain(z, own_tiles(starts[2], starts[3])), Chain(z, own_tiles(starts[3], starts[4]))
            one.run(1)
            two.run(1)
            one.grads, accs = compute(0, tiles, 0, None, (one.from_left[0], one.from_right[0]))
            one.run(1)
            after = (two.from_left[0], two.from_right[0], one.grads[3])
            two.grads, accs = compute(1, tiles, starts[1], accs, after)
            one.run(nz - 2)
            grads, accs = compute(2, all_tiles(one.slots()), 0, accs)
            three = Chain(z, None, grads)
            two.run(nz - 1)
            grads, accs = compute(3, all_tiles(two.slots()), 0, accs, (grads[3],))
            four = Chain(z, None, grads)
            sums = [one.total(), two.total(), three.run(nz - 1).total(), four.run(nz - 1).total()]

        output, input_grad = sum_columns(accs)
        weight_grads = [jnp.concatenate([jnp.swapaxes(g[kind], 1, 2) for g in sums], axis=0) for kind in range(3)]
        return (output, input_grad, *weight_grads)

    return shards


def solution(mesh):
    in_specs = (
        P("row", "col"),
        P("row", "col"),
        P("col", "row", None),
        P("col", "row", None),
        P("col", "row", None),
        P("col", None),
        P("col", None),
        P("col", None),
    )
    out_specs = in_specs[:5]
    shards = make_shards(mesh.shape["row"], mesh.shape["col"])
    return jax.shard_map(shards, mesh=mesh, in_specs=in_specs, out_specs=out_specs, check_vma=False)
```

```python
import functools

import jax
import jax.numpy as jnp
from jax import lax
from jax.experimental import pallas as pl
from jax.experimental.pallas import tpu as pltpu
from jax.sharding import PartitionSpec as P

BS = 128
BF = jnp.bfloat16
F32 = jnp.float32


def contract(a, b, da, db):
    return lax.dot_general(a, b, (((da,), (db,)), ((), ())), preferred_element_type=F32)


def chunk_kernel(scal, *refs, n_col, pieces, groups, waits, kg, f_total, f_first, blocks, first, last):
    refs = list(refs)

    def take(count):
        got = refs[:count]
        del refs[:count]
        return got

    (panels,) = take(1)
    take(waits)
    acc_in = [] if first else take(2)
    tiles = take(groups)
    tile_grads = take(groups)
    results = take(len(pieces)) if last else take(2)
    x_all, y_all, acc_out, acc_x, load_sem, acc_sem, store_sem = refs

    step = pl.program_id(0)
    steps = pl.num_programs(0)
    tokens = x_all.shape[1]
    order = 3 * f_total * kg
    me = scal[order + kg]
    both = (x_all, y_all)
    totals = (acc_out, acc_x)

    x_loads, y_loads = [
        [pltpu.make_async_copy(panels.at[slot, kind], both[kind].at[slot], load_sem.at[kind, slot]) for slot in range(n_col)]
        for kind in range(2)
    ]
    acc_loads = [pltpu.make_async_copy(src, dst, acc_sem.at[i]) for i, (src, dst) in enumerate(zip(acc_in, totals))]

    @pl.when(step == 0)
    def _():
        for copy in x_loads + y_loads + acc_loads:
            copy.start()
        if first:
            for total in totals:
                total[...] = jnp.zeros_like(total)
        for copy in x_loads:
            copy.wait()

    def places(table):
        found = []
        for s in range(kg):
            block = scal[table * f_total * kg + (f_first + step) * kg + scal[order + s]]
            found.append((block // blocks, pl.multiple_of(lax.rem(block, blocks) * BS, BS)))
        return found

    def picked(source, where):
        return jnp.concatenate([source[slot, :, pl.ds(at, BS)] for slot, at in where], axis=1)

    def stacked(kind):
        return jnp.concatenate([tile[i, kind, 0] for tile in tiles for i in range(tile.shape[0])], axis=0)

    def put(kind, grads):
        s = 0
        for ref in tile_grads:
            for i in range(ref.shape[0]):
                ref[i, kind, 0] = grads[:, s * BS : (s + 1) * BS].astype(BF)
                s += 1

    def scatter(total, where, left, right):
        for s in range(0, kg, 2):
            two = contract(left, right[s * BS : (s + 2) * BS], 1, 1)
            for i in range(2):
                slot, at = where[s + i]
                total[slot ^ me, :, pl.ds(at, BS)] += two[:, i * BS : (i + 1) * BS]

    gate_at, up_at, down_at = places(0), places(1), places(2)
    gate_w, up_w, down_w = stacked(0), stacked(1), stacked(2)
    x_gate, x_up = picked(x_all, gate_at), picked(x_all, up_at)
    gate = contract(x_gate, gate_w, 1, 0)
    up = contract(x_up, up_w, 1, 0)
    sig = jax.nn.sigmoid(gate)
    silu = gate * sig
    hidden = (silu * up).astype(BF)

    @pl.when(step == 0)
    def _():
        for copy in y_loads:
            copy.wait()

    y_down = picked(y_all, down_at)
    hidden_grad = contract(y_down, down_w, 1, 0)
    gate_grad = (hidden_grad * up * sig * (1.0 + gate * (1.0 - sig))).astype(BF)
    up_grad = (hidden_grad * silu).astype(BF)
    put(2, contract(hidden, y_down, 0, 0))
    put(0, contract(gate_grad, x_gate, 0, 0))
    put(1, contract(up_grad, x_up, 0, 0))

    @pl.when(step == 0)
    def _():
        for copy in acc_loads:
            copy.wait()

    scatter(acc_out, down_at, hidden, down_w)
    scatter(acc_x, gate_at, gate_grad, gate_w)
    scatter(acc_x, up_at, up_grad, up_w)

    @pl.when(step == steps - 1)
    def _():
        stores = []
        for kind, (total, rounded) in enumerate(zip(totals, both)):
            if last:
                for s in range(n_col):
                    for t in range(0, tokens, 32):
                        rounded[s, t : t + 32] = total[s, t : t + 32].astype(BF)
                here = [
                    pltpu.make_async_copy(
                        rounded.at[slot, pl.ds(at, rows)], results[p].at[kind], store_sem.at[kind, p]
                    )
                    for p, (slot, at, rows) in enumerate(pieces)
                ]
            else:
                here = [pltpu.make_async_copy(total, results[kind], acc_sem.at[kind])]
            for copy in here:
                copy.start()
            stores += here
        for copy in stores:
            copy.wait()


def run_chunk(scal, panels, after, pieces, accs, tiles, *, f_total, f_first, f_here, tile_first, last):
    n_col, _, tokens, width = panels.shape
    kg = sum(t.shape[0] for t in tiles)
    first = accs is None
    anywhere = pl.BlockSpec(memory_space=pl.ANY)
    tile_specs = [pl.BlockSpec((t.shape[0], 3, 1, BS, BS), lambda f, scal: (0, 0, f + tile_first, 0, 0)) for t in tiles]
    grad_specs = [pl.BlockSpec((t.shape[0], 3, 1, BS, BS), lambda f, scal: (0, 0, f, 0, 0)) for t in tiles]
    grad_shapes = [jax.ShapeDtypeStruct((t.shape[0], 3, f_here, BS, BS), BF) for t in tiles]
    if last:
        results = [jax.ShapeDtypeStruct((2, rows, width), BF) for _, _, rows in pieces]
    else:
        results = [jax.ShapeDtypeStruct((n_col, tokens, width), F32)] * 2
    kernel = functools.partial(
        chunk_kernel,
        n_col=n_col,
        pieces=pieces,
        groups=len(tiles),
        waits=len(after),
        kg=kg,
        f_total=f_total,
        f_first=f_first,
        blocks=width // BS,
        first=first,
        last=last,
    )
    flops = 9 * 2 * tokens * f_here * kg * BS * BS
    out = pl.pallas_call(
        kernel,
        grid_spec=pltpu.PrefetchScalarGridSpec(
            num_scalar_prefetch=1,
            grid=(f_here,),
            in_specs=[anywhere] * (1 + len(after) + (0 if first else 2)) + tile_specs,
            out_specs=grad_specs + [anywhere] * len(results),
            scratch_shapes=[
                pltpu.VMEM((n_col, tokens, width), BF),
                pltpu.VMEM((n_col, tokens, width), BF),
                pltpu.VMEM((n_col, tokens, width), F32),
                pltpu.VMEM((n_col, tokens, width), F32),
                pltpu.SemaphoreType.DMA((2, n_col)),
                pltpu.SemaphoreType.DMA((2,)),
                pltpu.SemaphoreType.DMA((2, len(pieces))),
            ],
        ),
        out_shape=grad_shapes + results,
        compiler_params=pltpu.CompilerParams(vmem_limit_bytes=48 * 1024 * 1024),
        cost_estimate=pl.CostEstimate(flops=flops, bytes_accessed=64 * 1024 * 1024, transcendentals=0),
        name="ffn_chunk",
    )(scal, panels, *after, *([] if first else accs), *tiles)
    return out[: len(tiles)], out[len(tiles) :]


def total_of(*terms):
    value = terms[0].astype(F32)
    for term in terms[1:]:
        value = value + term.astype(F32)
    return value.astype(BF)


def make_shards(n_row, n_col):
    nz = n_row // 2
    across = [(r, r ^ 1) for r in range(n_row)]
    two_phase = n_col == 4

    def right(first, stop):
        return [(2 * z + c, 2 * z + 2 + c) for z in range(first, stop) for c in (0, 1)]

    def left(first, stop):
        return [(2 * z + c, 2 * z - 2 + c) for z in range(first, stop) for c in (0, 1)]

    def over(value, offset):
        return lax.ppermute(value, "col", [(i, i ^ offset) for i in range(n_col)])

    def swap(value):
        return lax.ppermute(value, "row", across)

    def pieces_of(tokens):
        half = tokens // 2
        if two_phase:
            return ((0, 0, tokens), (1, 0, tokens), (2, 0, tokens), (3, 0, half), (3, half, half))
        return tuple((s, 0, tokens) for s in range(n_col))

    def sum_columns(parts):
        if two_phase:
            mine, beside, above, low, high = parts
            half = low.shape[1]
            low, high = over(low, 1), over(high, 2)
            above = jnp.concatenate([total_of(above[:, :half], low), above[:, half:]], axis=1)
            beside = jnp.concatenate([beside[:, :half], total_of(beside[:, half:], high)], axis=1)
            got = [over(beside, 1), over(above, 2)]
        else:
            mine = parts[0]
            got = [over(parts[o], o) for o in range(1, n_col)]
        return [total_of(mine[i], *[g[i] for g in got]) for i in range(2)]

    class Chain:
        def __init__(self, z, own=None, grads=None):
            self.z, self.own, self.grads = z, own, grads
            self.from_left, self.from_right = [], []
            self.tick = 0 if own is not None else 1

        def part(self, slot):
            return [g[slot // 2] for g in self.grads[slot % 2 :: 2]]

        def run(self, count):
            for _ in range(count):
                i = self.tick
                summing = self.grads is not None
                if i == 0:
                    to_right = to_left = self.own
                elif not summing:
                    to_right, to_left = self.from_left[-1], self.from_right[-1]
                else:
                    to_right = total_of(*self.part(i), *self.from_left[-1:])
                    to_left = total_of(*self.part(nz - i), *self.from_right[-1:])
                    if self.own is not None:
                        to_right = jnp.where(self.z >= i, self.from_left[-1], to_right)
                        to_left = jnp.where(nz - 1 - self.z >= i, self.from_right[-1], to_left)
                start = 0 if summing else i
                stop = nz - 1 if self.own is not None else i
                self.from_left.append(lax.ppermute(to_right, "row", right(start, stop)))
                self.from_right.append(lax.ppermute(to_left, "row", left(nz - stop, nz - start)))
                self.tick += 1
            return self

        def slots(self):
            found = [self.own]
            for o in range(1, nz):
                found.append(jnp.where(self.z >= o, self.from_left[o - 1], self.from_right[nz - o - 1]))
            return found

        def total(self):
            return total_of(*self.part(0), self.from_left[-1], self.from_right[-1])

    class Halves:
        def __init__(self, z, grads):
            self.even_z = z % 2 == 0
            self.grads = grads
            self.near = lax.ppermute(total_of(grads[1], grads[3]), "row", [(r, r ^ 2) for r in range(n_row)])

        def total(self):
            keep, _, got, _ = self.grads
            far = jnp.where(self.even_z, self.near[1], self.near[0])
            mine = jnp.where(self.even_z, self.near[0], self.near[1])
            rest = lax.ppermute(total_of(keep[1], got[1], far), "row", [(r, r ^ 4) for r in range(n_row)])
            return total_of(keep[0], got[0], mine, rest)

    def shards(tokens, out_grad, gate_weight, up_weight, down_weight, gate_rows, up_rows, down_columns):
        f_total, part = gate_weight.shape[:2]
        kg = gate_rows.shape[1]
        row = lax.axis_index("row")
        z, core = row // 2, row % 2
        whole_tiles = part == BS
        slots = list(range(0, nz, 2)) + list(range(1, nz, 2))
        spots = (z - jnp.array(slots, dtype=jnp.int32)) % nz
        order = jnp.concatenate([2 * spots + core, 2 * spots + 1 - core]) if whole_tiles else spots
        scal = jnp.concatenate(
            [t.reshape(-1) for t in (gate_rows, up_rows, down_columns)]
            + [order.astype(jnp.int32), lax.axis_index("col").astype(jnp.int32).reshape(1)]
        )
        pieces = pieces_of(tokens.shape[0])
        panels = lax.all_gather(jnp.stack([tokens, out_grad]), "col")

        def own_tiles(start, stop):
            return jnp.stack([w[start:stop] for w in (gate_weight, up_weight, down_weight)])

        def all_tiles(mine):
            even, odd = jnp.stack(mine[0::2]), jnp.stack(mine[1::2])
            other_even, other_odd = swap(even), swap(odd)
            if whole_tiles:
                return [even, odd, other_even, other_odd]
            return [
                jnp.where(core == 0, jnp.concatenate([a, b], -2), jnp.concatenate([b, a], -2))
                for a, b in ((even, other_even), (odd, other_odd))
            ]

        def exchanged(tile_grads, hold):
            if whole_tiles:
                keep, give = tile_grads[:2], tile_grads[2:]
            else:
                keep = [lax.dynamic_slice_in_dim(g, core * part, part, 4) for g in tile_grads]
                give = [lax.dynamic_slice_in_dim(g, (1 - core) * part, part, 4) for g in tile_grads]
            give, _ = lax.optimization_barrier((give, hold))
            got_odd = swap(give[1])
            return [keep[0], keep[1], swap(give[0]), got_odd]

        if f_total % 4 == 0 and nz == 4 and whole_tiles:
            sizes = [f_total // 4] * 4
        else:
            sizes = [f_total]
        starts = [sum(sizes[:i]) for i in range(len(sizes) + 1)]
        accs = None

        def compute(i, tiles, tile_first, accs, after=(), hold=()):
            tile_grads, accs = run_chunk(
                scal,
                panels,
                after,
                pieces,
                accs,
                tiles,
                f_total=f_total,
                f_first=starts[i],
                f_here=sizes[i],
                tile_first=tile_first,
                last=i == len(sizes) - 1,
            )
            return exchanged(tile_grads, hold), accs

        if len(sizes) == 1:
            gather = Chain(z, own_tiles(0, f_total)).run(nz - 1)
            grads, accs = compute(0, all_tiles(gather.slots()), 0, None)
            sums = [Chain(z, None, grads).run(nz - 1).total()]
        else:
            gather = Chain(z, own_tiles(0, starts[2])).run(nz - 1)
            tiles = all_tiles(gather.slots())
            one, two = Chain(z, own_tiles(starts[2], starts[3])), Chain(z, own_tiles(starts[3], starts[4]))
            one.run(1)
            two.run(1)
            hold = (one.from_left[0], one.from_right[0], two.from_left[0], two.from_right[0])
            one.grads, accs = compute(0, tiles, 0, None, (), hold)
            one.run(1)
            two.grads, accs = compute(1, tiles, starts[1], accs, (one.grads[3],), (one.from_left[1], one.from_right[1]))
            one.run(1)
            two.run(1)
            mine = one.slots()
            one.run(nz - 3)
            two.run(1)
            hold = (one.from_left[3], one.from_right[3], two.from_left[2], two.from_right[2])
            grads, accs = compute(2, all_tiles(mine), 0, accs, (), hold)
            three = Halves(z, grads)
            last, accs = compute(3, all_tiles(two.slots()), 0, accs, (grads[3],), (three.near,))
            two.run(nz - 3)
            sums = [one.total(), two.total(), three.total(), Halves(z, last).total()]

        output, input_grad = sum_columns(accs)
        weight_grads = [jnp.concatenate([jnp.swapaxes(g[kind], 1, 2) for g in sums], axis=0) for kind in range(3)]
        return (output, input_grad, *weight_grads)

    return shards


def solution(mesh):
    in_specs = (
        P("row", "col"),
        P("row", "col"),
        P("col", "row", None),
        P("col", "row", None),
        P("col", "row", None),
        P("col", None),
        P("col", None),
        P("col", None),
    )
    out_specs = in_specs[:5]
    shards = make_shards(mesh.shape["row"], mesh.shape["col"])
    return jax.shard_map(shards, mesh=mesh, in_specs=in_specs, out_specs=out_specs, check_vma=False)
```

```python
import functools

import jax
import jax.numpy as jnp
from jax import lax
from jax.experimental import pallas as pl
from jax.experimental.pallas import tpu as pltpu
from jax.sharding import PartitionSpec as P

BS = 128
BF = jnp.bfloat16
F32 = jnp.float32


def contract(a, b, da, db):
    return lax.dot_general(a, b, (((da,), (db,)), ((), ())), preferred_element_type=F32)


def taker(refs):
    refs = list(refs)

    def take(count):
        got = refs[:count]
        del refs[:count]
        return got

    return take


def places(scal, table, f, *, kg, f_total, blocks):
    found = []
    for s in range(kg):
        block = scal[table * f_total * kg + f * kg + scal[3 * f_total * kg + s]]
        found.append((block // blocks, pl.multiple_of(lax.rem(block, blocks) * BS, BS)))
    return found


def stacked(tiles, kind, j):
    return jnp.concatenate([tile[i, kind, j] for tile in tiles for i in range(tile.shape[0])], axis=0)


def grad_kernel(scal, *refs, n_col, groups, waits, per, kg, f_total, f_first, blocks):
    take = taker(refs)
    (panels,) = take(1)
    take(waits)
    tiles = take(groups)
    tile_grads = take(groups)
    stash, x_all, y_all, load_sem = take(4)
    step = pl.program_id(0)
    both = (x_all, y_all)
    loads = [
        [pltpu.make_async_copy(panels.at[slot, kind], both[kind].at[slot], load_sem.at[kind, slot]) for slot in range(n_col)]
        for kind in range(2)
    ]

    def picked(source, table, j):
        where = places(scal, table, f_first + step * per + j, kg=kg, f_total=f_total, blocks=blocks)
        return jnp.concatenate([source[slot, :, pl.ds(at, BS)] for slot, at in where], axis=1)

    def put(kind, j, grads):
        s = 0
        for ref in tile_grads:
            for i in range(ref.shape[0]):
                ref[i, kind, j] = grads[:, s * BS : (s + 1) * BS].astype(BF)
                s += 1

    def body(before_y):
        fs = range(per)
        x_gate = [picked(x_all, 0, j) for j in fs]
        x_up = [picked(x_all, 1, j) for j in fs]
        gates = [contract(x_gate[j], stacked(tiles, 0, j), 1, 0) for j in fs]
        ups = [contract(x_up[j], stacked(tiles, 1, j), 1, 0) for j in fs]
        before_y()
        y_down = [picked(y_all, 2, j) for j in fs]
        downs = [contract(y_down[j], stacked(tiles, 2, j), 1, 0) for j in fs]
        for j in fs:
            gate, up, hidden_grad = gates[j], ups[j], downs[j]
            sig = jax.nn.sigmoid(gate)
            silu = gate * sig
            hidden = (silu * up).astype(BF)
            gate_grad = (hidden_grad * up * sig * (1.0 + gate * (1.0 - sig))).astype(BF)
            up_grad = (hidden_grad * silu).astype(BF)
            for kind, value in enumerate((gate_grad, up_grad, hidden)):
                stash[kind, j] = value
            put(2, j, contract(hidden, y_down[j], 0, 0))
            put(0, j, contract(gate_grad, x_gate[j], 0, 0))
            put(1, j, contract(up_grad, x_up[j], 0, 0))

    @pl.when(step == 0)
    def _():
        for copy in loads[0] + loads[1]:
            copy.start()
        for copy in loads[0]:
            copy.wait()

        def wait_y():
            for copy in loads[1]:
                copy.wait()

        body(wait_y)

    @pl.when(step > 0)
    def _():
        body(lambda: None)


def run_grads(scal, panels, after, tiles, *, f_total, f_first, f_here, tile_first):
    n_col, _, tokens, width = panels.shape
    kg = sum(t.shape[0] for t in tiles)
    per = 2 if f_here % 2 == 0 and tile_first % 2 == 0 else 1
    anywhere = pl.BlockSpec(memory_space=pl.ANY)

    def tile_spec(t, first):
        return pl.BlockSpec((t.shape[0], 3, per, BS, BS), lambda f, scal: (0, 0, f + first, 0, 0))

    kernel = functools.partial(
        grad_kernel,
        n_col=n_col,
        groups=len(tiles),
        waits=len(after),
        per=per,
        kg=kg,
        f_total=f_total,
        f_first=f_first,
        blocks=width // BS,
    )
    out = pl.pallas_call(
        kernel,
        grid_spec=pltpu.PrefetchScalarGridSpec(
            num_scalar_prefetch=1,
            grid=(f_here // per,),
            in_specs=[anywhere] * (1 + len(after)) + [tile_spec(t, tile_first // per) for t in tiles],
            out_specs=[tile_spec(t, 0) for t in tiles]
            + [pl.BlockSpec((3, per, tokens, BS), lambda f, scal: (0, f, 0, 0))],
            scratch_shapes=[
                pltpu.VMEM((n_col, tokens, width), BF),
                pltpu.VMEM((n_col, tokens, width), BF),
                pltpu.SemaphoreType.DMA((2, n_col)),
            ],
        ),
        out_shape=[jax.ShapeDtypeStruct((t.shape[0], 3, f_here, BS, BS), BF) for t in tiles]
        + [jax.ShapeDtypeStruct((3, f_here, tokens, BS), BF)],
        compiler_params=pltpu.CompilerParams(vmem_limit_bytes=48 * 1024 * 1024),
        cost_estimate=pl.CostEstimate(
            flops=6 * 2 * tokens * f_here * kg * BS * BS, bytes_accessed=f_here * 6 * 1024 * 1024, transcendentals=0
        ),
        name="ffn_grads",
    )(scal, panels, *after, *tiles)
    return out[: len(tiles)], out[-1]


def add_kernel(scal, *refs, n_col, pieces, groups, waits, segments, per, kg, f_total, blocks, first, last):
    take = taker(refs)
    take(waits)
    acc_in = [] if first else take(2)
    parts = [(take(1)[0], take(groups)) for _ in segments]
    results = take(len(pieces)) if last else take(2)
    totals = take(2)
    rounded = take(2) if last else []
    acc_sem, store_sem = take(2)
    step = pl.program_id(0)
    me = scal[3 * f_total * kg + kg]
    acc_loads = [pltpu.make_async_copy(src, dst, acc_sem.at[i]) for i, (src, dst) in enumerate(zip(acc_in, totals))]

    def scatter(total, where, left, right):
        for s in range(0, kg, 2):
            two = contract(left, right[s * BS : (s + 2) * BS], 1, 1)
            for i in range(2):
                slot, at = where[s + i]
                total[slot ^ me, :, pl.ds(at, BS)] += two[:, i * BS : (i + 1) * BS]

    @pl.when(step == 0)
    def _():
        for copy in acc_loads:
            copy.start()
        if first:
            for total in totals:
                total[...] = jnp.zeros_like(total)
        for copy in acc_loads:
            copy.wait()

    before = 0
    for (f_first, _, steps), (stash, tiles) in zip(segments, parts):

        @pl.when((step >= before) & (step < before + steps))
        def _():
            for j in range(per):
                f = f_first + (step - before) * per + j
                for kind, total in ((2, totals[0]), (0, totals[1]), (1, totals[1])):
                    where = places(scal, kind, f, kg=kg, f_total=f_total, blocks=blocks)
                    scatter(total, where, stash[kind, j], stacked(tiles, kind, j))

        before += steps

    @pl.when(step == before - 1)
    def _():
        stores = []
        for kind, total in enumerate(totals):
            if last:
                for s in range(n_col):
                    for t in range(0, total.shape[1], 32):
                        rounded[kind][s, t : t + 32] = total[s, t : t + 32].astype(BF)
                    here = [
                        pltpu.make_async_copy(
                            rounded[kind].at[slot, pl.ds(at, rows)], results[p].at[kind], store_sem.at[kind, p]
                        )
                        for p, (slot, at, rows) in enumerate(pieces)
                        if slot == s
                    ]
                    for copy in here:
                        copy.start()
                    stores += here
            else:
                copy = pltpu.make_async_copy(total, results[kind], acc_sem.at[kind])
                copy.start()
                stores.append(copy)
        for copy in stores:
            copy.wait()


def run_adds(scal, accs, after, parts, pieces, *, n_col, width, f_total, last):
    tokens = parts[0][1].shape[2]
    kg = sum(t.shape[0] for t in parts[0][2])
    first = accs is None
    anywhere = pl.BlockSpec(memory_space=pl.ANY)
    per = 2 if all(stash.shape[1] % 2 == 0 and at % 2 == 0 for _, stash, _, at in parts) else 1
    segments, specs, operands, before = [], [], [], 0
    for f_first, stash, tiles, at in parts:
        steps = stash.shape[1] // per

        def spot(f, before=before, steps=steps):
            return jnp.clip(f - before, 0, steps - 1)

        specs.append(pl.BlockSpec((3, per, tokens, BS), lambda f, scal, spot=spot: (0, spot(f), 0, 0)))
        for t in tiles:
            specs.append(
                pl.BlockSpec(
                    (t.shape[0], 3, per, BS, BS),
                    lambda f, scal, spot=spot, start=at // per: (0, 0, spot(f) + start, 0, 0),
                )
            )
        operands += [stash, *tiles]
        segments.append((f_first, at, steps))
        before += steps
    acc_shape = (n_col, tokens, width)
    if last:
        results = [jax.ShapeDtypeStruct((2, rows, width), BF) for _, _, rows in pieces]
    else:
        results = [jax.ShapeDtypeStruct(acc_shape, F32)] * 2
    kernel = functools.partial(
        add_kernel,
        n_col=n_col,
        pieces=pieces,
        groups=len(parts[0][2]),
        waits=len(after),
        segments=segments,
        per=per,
        kg=kg,
        f_total=f_total,
        blocks=width // BS,
        first=first,
        last=last,
    )
    return pl.pallas_call(
        kernel,
        grid_spec=pltpu.PrefetchScalarGridSpec(
            num_scalar_prefetch=1,
            grid=(before,),
            in_specs=[anywhere] * (len(after) + (0 if first else 2)) + specs,
            out_specs=[anywhere] * len(results),
            scratch_shapes=[pltpu.VMEM(acc_shape, F32)] * 2
            + ([pltpu.VMEM(acc_shape, BF)] * 2 if last else [])
            + [pltpu.SemaphoreType.DMA((2,)), pltpu.SemaphoreType.DMA((2, len(pieces)))],
        ),
        out_shape=results,
        compiler_params=pltpu.CompilerParams(vmem_limit_bytes=56 * 1024 * 1024),
        cost_estimate=pl.CostEstimate(
            flops=3 * 2 * tokens * before * per * kg * BS * BS, bytes_accessed=48 * 1024 * 1024, transcendentals=0
        ),
        name="ffn_adds",
    )(scal, *after, *([] if first else accs), *operands)


def total_of(*terms):
    value = terms[0].astype(F32)
    for term in terms[1:]:
        value = value + term.astype(F32)
    return value.astype(BF)


def make_shards(n_row, n_col):
    nz = n_row // 2
    across = [(r, r ^ 1) for r in range(n_row)]
    two_phase = n_col == 4

    def right(first, stop):
        return [(2 * z + c, 2 * z + 2 + c) for z in range(first, stop) for c in (0, 1)]

    def left(first, stop):
        return [(2 * z + c, 2 * z - 2 + c) for z in range(first, stop) for c in (0, 1)]

    def over(value, offset):
        return lax.ppermute(value, "col", [(i, i ^ offset) for i in range(n_col)])

    def swap(value):
        return lax.ppermute(value, "row", across)

    def pieces_of(tokens):
        half = tokens // 2
        if two_phase:
            return ((0, 0, tokens), (1, 0, tokens), (2, 0, tokens), (3, 0, half), (3, half, half))
        return tuple((s, 0, tokens) for s in range(n_col))

    def sum_columns(parts):
        if two_phase:
            mine, beside, above, low, high = parts
            half = low.shape[1]
            low, high = over(low, 1), over(high, 2)
            above = jnp.concatenate([total_of(above[:, :half], low), above[:, half:]], axis=1)
            beside = jnp.concatenate([beside[:, :half], total_of(beside[:, half:], high)], axis=1)
            got = [over(beside, 1), over(above, 2)]
        else:
            mine = parts[0]
            got = [over(parts[o], o) for o in range(1, n_col)]
        return [total_of(mine[i], *[g[i] for g in got]) for i in range(2)]

    class Chain:
        def __init__(self, z, own=None, grads=None):
            self.z, self.own, self.grads = z, own, grads
            self.from_left, self.from_right = [], []
            self.tick = 0 if own is not None else 1

        def part(self, slot):
            return [g[slot // 2] for g in self.grads[slot % 2 :: 2]]

        def run(self, count):
            for _ in range(count):
                i = self.tick
                summing = self.grads is not None
                if i == 0:
                    to_right = to_left = self.own
                elif not summing:
                    to_right, to_left = self.from_left[-1], self.from_right[-1]
                else:
                    to_right = total_of(*self.part(i), *self.from_left[-1:])
                    to_left = total_of(*self.part(nz - i), *self.from_right[-1:])
                    if self.own is not None:
                        to_right = jnp.where(self.z >= i, self.from_left[-1], to_right)
                        to_left = jnp.where(nz - 1 - self.z >= i, self.from_right[-1], to_left)
                start = 0 if summing else i
                stop = nz - 1 if self.own is not None else i
                self.from_left.append(lax.ppermute(to_right, "row", right(start, stop)))
                self.from_right.append(lax.ppermute(to_left, "row", left(nz - stop, nz - start)))
                self.tick += 1
            return self

        def slots(self):
            found = [self.own]
            for o in range(1, nz):
                found.append(jnp.where(self.z >= o, self.from_left[o - 1], self.from_right[nz - o - 1]))
            return found

        def total(self):
            return total_of(*self.part(0), self.from_left[-1], self.from_right[-1])

    class Halves:
        def __init__(self, z, grads):
            self.even_z = z % 2 == 0
            self.grads = grads
            self.near = lax.ppermute(total_of(grads[1], grads[3]), "row", [(r, r ^ 2) for r in range(n_row)])

        def total(self):
            keep, _, got, _ = self.grads
            far = jnp.where(self.even_z, self.near[1], self.near[0])
            mine = jnp.where(self.even_z, self.near[0], self.near[1])
            rest = lax.ppermute(total_of(keep[1], got[1], far), "row", [(r, r ^ 4) for r in range(n_row)])
            return total_of(keep[0], got[0], mine, rest)

    def shards(tokens, out_grad, gate_weight, up_weight, down_weight, gate_rows, up_rows, down_columns):
        f_total, part = gate_weight.shape[:2]
        kg = gate_rows.shape[1]
        row = lax.axis_index("row")
        z, core = row // 2, row % 2
        whole_tiles = part == BS
        slots = list(range(0, nz, 2)) + list(range(1, nz, 2))
        spots = (z - jnp.array(slots, dtype=jnp.int32)) % nz
        order = jnp.concatenate([2 * spots + core, 2 * spots + 1 - core]) if whole_tiles else spots
        scal = jnp.concatenate(
            [t.reshape(-1) for t in (gate_rows, up_rows, down_columns)]
            + [order.astype(jnp.int32), lax.axis_index("col").astype(jnp.int32).reshape(1)]
        )
        pieces = pieces_of(tokens.shape[0])
        panels = lax.all_gather(jnp.stack([tokens, out_grad]), "col")

        def own_tiles(start, stop):
            return jnp.stack([w[start:stop] for w in (gate_weight, up_weight, down_weight)])

        def all_tiles(mine):
            even, odd = jnp.stack(mine[0::2]), jnp.stack(mine[1::2])
            other_even, other_odd = swap(even), swap(odd)
            if whole_tiles:
                return [even, odd, other_even, other_odd]
            return [
                jnp.where(core == 0, jnp.concatenate([a, b], -2), jnp.concatenate([b, a], -2))
                for a, b in ((even, other_even), (odd, other_odd))
            ]

        def exchanged(tile_grads, hold):
            if whole_tiles:
                keep, give = tile_grads[:2], tile_grads[2:]
            else:
                keep = [lax.dynamic_slice_in_dim(g, core * part, part, 4) for g in tile_grads]
                give = [lax.dynamic_slice_in_dim(g, (1 - core) * part, part, 4) for g in tile_grads]
            give, _ = lax.optimization_barrier((give, hold))
            got_odd = swap(give[1])
            return [keep[0], keep[1], swap(give[0]), got_odd]

        width = tokens.shape[1]

        def compute(f_first, f_here, tiles, tile_first, after=(), hold=()):
            tile_grads, stash = run_grads(
                scal, panels, after, tiles, f_total=f_total, f_first=f_first, f_here=f_here, tile_first=tile_first
            )
            return exchanged(tile_grads, hold), (f_first, stash, tiles, tile_first)

        def add_up(accs, parts, last, after=()):
            return run_adds(scal, accs, after, parts, pieces, n_col=n_col, width=width, f_total=f_total, last=last)

        if f_total % 4 == 0 and nz == 4 and whole_tiles:
            half = f_total // 2
            big = half // 2 + half // 2 % 2
            small = half - big
            second, third, fourth = big, half, half + big
            tiles = all_tiles(Chain(z, own_tiles(0, half)).run(3).slots())
            one, two = Chain(z, own_tiles(third, fourth)).run(1), Chain(z, own_tiles(fourth, f_total)).run(1)
            hold = (one.from_left[0], one.from_right[0], two.from_left[0], two.from_right[0])
            one.grads, part_0 = compute(0, big, tiles, 0, (), hold)
            one.run(1)
            two.grads, part_1 = compute(
                second, small, tiles, second, (one.grads[3],), (one.from_left[1], one.from_right[1])
            )
            accs = add_up(None, [part_0, part_1], False)
            one.from_left[1], one.from_right[1], _ = lax.optimization_barrier(
                (one.from_left[1], one.from_right[1], two.grads[3])
            )
            one.run(1)
            two.run(1)
            mine = one.slots()
            one.run(1)
            two.run(1)
            hold = (one.from_left[3], one.from_right[3], two.from_left[2], two.from_right[2])
            grads, part_2 = compute(third, big, all_tiles(mine), 0, (accs[0],), hold)
            three = Halves(z, grads)
            last, part_3 = compute(fourth, small, all_tiles(two.slots()), 0, (grads[3],))
            accs = add_up(accs, [part_2, part_3], True, (last[3],))
            two.run(1)
            sums = [one.total(), two.total(), three.total(), Halves(z, last).total()]
        else:
            gather = Chain(z, own_tiles(0, f_total)).run(nz - 1)
            grads, part_0 = compute(0, f_total, all_tiles(gather.slots()), 0)
            accs = add_up(None, [part_0], True)
            sums = [Chain(z, None, grads).run(nz - 1).total()]

        output, input_grad = sum_columns(accs)
        weight_grads = [jnp.concatenate([jnp.swapaxes(g[kind], 1, 2) for g in sums], axis=0) for kind in range(3)]
        return (output, input_grad, *weight_grads)

    return shards


def solution(mesh):
    in_specs = (
        P("row", "col"),
        P("row", "col"),
        P("col", "row", None),
        P("col", "row", None),
        P("col", "row", None),
        P("col", None),
        P("col", None),
        P("col", None),
    )
    out_specs = in_specs[:5]
    shards = make_shards(mesh.shape["row"], mesh.shape["col"])
    return jax.shard_map(shards, mesh=mesh, in_specs=in_specs, out_specs=out_specs, check_vma=False)
```

```python
import functools

import jax
import jax.numpy as jnp
from jax import lax
from jax.experimental import pallas as pl
from jax.experimental.pallas import tpu as pltpu
from jax.sharding import PartitionSpec as P

BS = 128
BF = jnp.bfloat16
F32 = jnp.float32


def contract(a, b, da, db):
    return lax.dot_general(a, b, (((da,), (db,)), ((), ())), preferred_element_type=F32)


def taker(refs):
    refs = list(refs)

    def take(count):
        got = refs[:count]
        del refs[:count]
        return got

    return take


def places(scal, table, f, *, kg, f_total, blocks):
    found = []
    for s in range(kg):
        block = scal[table * f_total * kg + f * kg + scal[3 * f_total * kg + s]]
        found.append((block // blocks, lax.rem(block, blocks)))
    return found


def stacked(tiles, kind, j):
    return jnp.concatenate([tile[i, kind, j] for tile in tiles for i in range(tile.shape[0])], axis=0)


def grad_kernel(scal, *refs, n_col, groups, waits, per, kg, f_total, f_first, blocks):
    take = taker(refs)
    (panels,) = take(1)
    take(waits)
    tiles = take(groups)
    tile_grads = take(groups)
    stash, x_all, y_all, load_sem = take(4)
    step = pl.program_id(0)
    both = (x_all, y_all)
    loads = [
        [pltpu.make_async_copy(panels.at[slot, kind], both[kind].at[slot], load_sem.at[kind, slot]) for slot in range(n_col)]
        for kind in range(2)
    ]

    def picked(source, table, j):
        where = places(scal, table, f_first + step * per + j, kg=kg, f_total=f_total, blocks=blocks)
        return jnp.concatenate([source[slot, :, pl.ds(pl.multiple_of(block * BS, BS), BS)] for slot, block in where], axis=1)

    def put(kind, j, grads):
        s = 0
        for ref in tile_grads:
            for i in range(ref.shape[0]):
                ref[i, kind, j] = grads[:, s * BS : (s + 1) * BS].astype(BF)
                s += 1

    def body(before_y):
        fs = range(per)
        x_gate = [picked(x_all, 0, j) for j in fs]
        x_up = [picked(x_all, 1, j) for j in fs]
        gates = [contract(x_gate[j], stacked(tiles, 0, j), 1, 0) for j in fs]
        ups = [contract(x_up[j], stacked(tiles, 1, j), 1, 0) for j in fs]
        before_y()
        y_down = [picked(y_all, 2, j) for j in fs]
        downs = [contract(y_down[j], stacked(tiles, 2, j), 1, 0) for j in fs]
        for j in fs:
            gate, up, hidden_grad = gates[j], ups[j], downs[j]
            sig = jax.nn.sigmoid(gate)
            silu = gate * sig
            hidden = (silu * up).astype(BF)
            gate_grad = (hidden_grad * up * sig * (1.0 + gate * (1.0 - sig))).astype(BF)
            up_grad = (hidden_grad * silu).astype(BF)
            for kind, value, source in ((2, hidden, y_down[j]), (0, gate_grad, x_gate[j]), (1, up_grad, x_up[j])):
                turned = value.T
                stash[kind, j] = turned
                put(kind, j, contract(turned, source, 1, 0))

    @pl.when(step == 0)
    def _():
        for copy in loads[0] + loads[1]:
            copy.start()
        for copy in loads[0]:
            copy.wait()

        def wait_y():
            for copy in loads[1]:
                copy.wait()

        body(wait_y)

    @pl.when(step > 0)
    def _():
        body(lambda: None)


def run_grads(scal, panels, after, tiles, *, f_total, f_first, f_here, tile_first):
    n_col, _, tokens, width = panels.shape
    kg = sum(t.shape[0] for t in tiles)
    per = 2 if f_here % 2 == 0 and tile_first % 2 == 0 else 1
    anywhere = pl.BlockSpec(memory_space=pl.ANY)

    def tile_spec(t, first):
        return pl.BlockSpec((t.shape[0], 3, per, BS, BS), lambda f, scal: (0, 0, f + first, 0, 0))

    kernel = functools.partial(
        grad_kernel,
        n_col=n_col,
        groups=len(tiles),
        waits=len(after),
        per=per,
        kg=kg,
        f_total=f_total,
        f_first=f_first,
        blocks=width // BS,
    )
    out = pl.pallas_call(
        kernel,
        grid_spec=pltpu.PrefetchScalarGridSpec(
            num_scalar_prefetch=1,
            grid=(f_here // per,),
            in_specs=[anywhere] * (1 + len(after)) + [tile_spec(t, tile_first // per) for t in tiles],
            out_specs=[tile_spec(t, 0) for t in tiles]
            + [pl.BlockSpec((3, per, BS, tokens), lambda f, scal: (0, f, 0, 0))],
            scratch_shapes=[
                pltpu.VMEM((n_col, tokens, width), BF),
                pltpu.VMEM((n_col, tokens, width), BF),
                pltpu.SemaphoreType.DMA((2, n_col)),
            ],
        ),
        out_shape=[jax.ShapeDtypeStruct((t.shape[0], 3, f_here, BS, BS), BF) for t in tiles]
        + [jax.ShapeDtypeStruct((3, f_here, BS, tokens), BF)],
        compiler_params=pltpu.CompilerParams(vmem_limit_bytes=48 * 1024 * 1024),
        cost_estimate=pl.CostEstimate(
            flops=6 * 2 * tokens * f_here * kg * BS * BS, bytes_accessed=f_here * 6 * 1024 * 1024, transcendentals=0
        ),
        name="ffn_grads",
    )(scal, panels, *after, *tiles)
    return out[: len(tiles)], out[-1]


def add_kernel(scal, *refs, n_col, pieces, groups, waits, segments, per, kg, f_total, blocks, first, last):
    take = taker(refs)
    take(waits)
    acc_in = [] if first else take(2)
    parts = [(take(1)[0], take(groups)) for _ in segments]
    results = take(len(pieces)) if last else take(2)
    totals = take(2)
    rounded = take(2) if last else []
    acc_sem, store_sem = take(2)
    step = pl.program_id(0)
    me = scal[3 * f_total * kg + kg]
    acc_loads = [pltpu.make_async_copy(src, dst, acc_sem.at[i]) for i, (src, dst) in enumerate(zip(acc_in, totals))]

    def scatter(total, where, tile_rows, turned):
        added = contract(tile_rows, turned, 1, 0)
        for s, (slot, block) in enumerate(where):
            total[(slot ^ me) * blocks + block] += added[s * BS : (s + 1) * BS]

    @pl.when(step == 0)
    def _():
        for copy in acc_loads:
            copy.start()
        if first:
            for total in totals:
                total[...] = jnp.zeros_like(total)
        for copy in acc_loads:
            copy.wait()

    before = 0
    for (f_first, _, steps), (stash, tiles) in zip(segments, parts):

        @pl.when((step >= before) & (step < before + steps))
        def _():
            for j in range(per):
                f = f_first + (step - before) * per + j
                for kind, total in ((2, totals[0]), (0, totals[1]), (1, totals[1])):
                    where = places(scal, kind, f, kg=kg, f_total=f_total, blocks=blocks)
                    scatter(total, where, stacked(tiles, kind, j), stash[kind, j])

        before += steps

    @pl.when(step == before - 1)
    def _():
        stores = []
        for kind, total in enumerate(totals):
            if last:
                for s in range(n_col):
                    for i in range(s * blocks, (s + 1) * blocks):
                        rounded[kind][i] = total[i].astype(BF)
                    here = [
                        pltpu.make_async_copy(
                            rounded[kind].at[pl.ds(slot * blocks + at, count)], results[p].at[kind], store_sem.at[kind, p]
                        )
                        for p, (slot, at, count) in enumerate(pieces)
                        if slot == s
                    ]
                    for copy in here:
                        copy.start()
                    stores += here
            else:
                copy = pltpu.make_async_copy(total, results[kind], acc_sem.at[kind])
                copy.start()
                stores.append(copy)
        for copy in stores:
            copy.wait()


def run_adds(scal, accs, after, parts, pieces, *, n_col, width, f_total, last):
    tokens = parts[0][1].shape[3]
    kg = sum(t.shape[0] for t in parts[0][2])
    first = accs is None
    anywhere = pl.BlockSpec(memory_space=pl.ANY)
    per = 2 if all(stash.shape[1] % 2 == 0 and at % 2 == 0 for _, stash, _, at in parts) else 1
    segments, specs, operands, before = [], [], [], 0
    for f_first, stash, tiles, at in parts:
        steps = stash.shape[1] // per

        def spot(f, before=before, steps=steps):
            return jnp.clip(f - before, 0, steps - 1)

        specs.append(pl.BlockSpec((3, per, BS, tokens), lambda f, scal, spot=spot: (0, spot(f), 0, 0)))
        for t in tiles:
            specs.append(
                pl.BlockSpec(
                    (t.shape[0], 3, per, BS, BS),
                    lambda f, scal, spot=spot, start=at // per: (0, 0, spot(f) + start, 0, 0),
                )
            )
        operands += [stash, *tiles]
        segments.append((f_first, at, steps))
        before += steps
    acc_shape = (n_col * width // BS, BS, tokens)
    if last:
        results = [jax.ShapeDtypeStruct((2, count, BS, tokens), BF) for _, _, count in pieces]
    else:
        results = [jax.ShapeDtypeStruct(acc_shape, F32)] * 2
    kernel = functools.partial(
        add_kernel,
        n_col=n_col,
        pieces=pieces,
        groups=len(parts[0][2]),
        waits=len(after),
        segments=segments,
        per=per,
        kg=kg,
        f_total=f_total,
        blocks=width // BS,
        first=first,
        last=last,
    )
    return pl.pallas_call(
        kernel,
        grid_spec=pltpu.PrefetchScalarGridSpec(
            num_scalar_prefetch=1,
            grid=(before,),
            in_specs=[anywhere] * (len(after) + (0 if first else 2)) + specs,
            out_specs=[anywhere] * len(results),
            scratch_shapes=[pltpu.VMEM(acc_shape, F32)] * 2
            + ([pltpu.VMEM(acc_shape, BF)] * 2 if last else [])
            + [pltpu.SemaphoreType.DMA((2,)), pltpu.SemaphoreType.DMA((2, len(pieces)))],
        ),
        out_shape=results,
        compiler_params=pltpu.CompilerParams(vmem_limit_bytes=56 * 1024 * 1024),
        cost_estimate=pl.CostEstimate(
            flops=3 * 2 * tokens * before * per * kg * BS * BS, bytes_accessed=48 * 1024 * 1024, transcendentals=0
        ),
        name="ffn_adds",
    )(scal, *after, *([] if first else accs), *operands)


def total_of(*terms):
    value = terms[0].astype(F32)
    for term in terms[1:]:
        value = value + term.astype(F32)
    return value.astype(BF)


def make_shards(n_row, n_col):
    nz = n_row // 2
    across = [(r, r ^ 1) for r in range(n_row)]
    two_phase = n_col == 4

    def right(first, stop):
        return [(2 * z + c, 2 * z + 2 + c) for z in range(first, stop) for c in (0, 1)]

    def left(first, stop):
        return [(2 * z + c, 2 * z - 2 + c) for z in range(first, stop) for c in (0, 1)]

    def over(value, offset):
        return lax.ppermute(value, "col", [(i, i ^ offset) for i in range(n_col)])

    def swap(value):
        return lax.ppermute(value, "row", across)

    def pieces_of(blocks):
        half = blocks // 2
        if two_phase:
            return ((0, 0, blocks), (1, 0, blocks), (2, 0, blocks), (3, 0, half), (3, half, blocks - half))
        return tuple((s, 0, blocks) for s in range(n_col))

    def sum_columns(parts):
        if two_phase:
            mine, beside, above, low, high = parts
            half = low.shape[1]
            low, high = over(low, 1), over(high, 2)
            above = jnp.concatenate([total_of(above[:, :half], low), above[:, half:]], axis=1)
            beside = jnp.concatenate([beside[:, :half], total_of(beside[:, half:], high)], axis=1)
            got = [over(beside, 1), over(above, 2)]
        else:
            mine = parts[0]
            got = [over(parts[o], o) for o in range(1, n_col)]
        sums = [total_of(mine[i], *[g[i] for g in got]) for i in range(2)]
        return [total.reshape(-1, total.shape[-1]).T for total in sums]

    class Chain:
        def __init__(self, z, own=None, grads=None):
            self.z, self.own, self.grads = z, own, grads
            self.from_left, self.from_right = [], []
            self.tick = 0 if own is not None else 1

        def part(self, slot):
            return [g[slot // 2] for g in self.grads[slot % 2 :: 2]]

        def run(self, count):
            for _ in range(count):
                i = self.tick
                summing = self.grads is not None
                if i == 0:
                    to_right = to_left = self.own
                elif not summing:
                    to_right, to_left = self.from_left[-1], self.from_right[-1]
                else:
                    to_right = total_of(*self.part(i), *self.from_left[-1:])
                    to_left = total_of(*self.part(nz - i), *self.from_right[-1:])
                    if self.own is not None:
                        to_right = jnp.where(self.z >= i, self.from_left[-1], to_right)
                        to_left = jnp.where(nz - 1 - self.z >= i, self.from_right[-1], to_left)
                start = 0 if summing else i
                stop = nz - 1 if self.own is not None else i
                self.from_left.append(lax.ppermute(to_right, "row", right(start, stop)))
                self.from_right.append(lax.ppermute(to_left, "row", left(nz - stop, nz - start)))
                self.tick += 1
            return self

        def received(self, i):
            return (self.from_left[i], self.from_right[i])

        def tie(self, i, other):
            self.from_left[i], self.from_right[i], _ = lax.optimization_barrier((*self.received(i), other))

        def slots(self):
            found = [self.own]
            for o in range(1, nz):
                found.append(jnp.where(self.z >= o, self.from_left[o - 1], self.from_right[nz - o - 1]))
            return found

        def total(self):
            return total_of(*self.part(0), self.from_left[-1], self.from_right[-1])

    class Halves:
        def __init__(self, z, grads):
            self.even_z = z % 2 == 0
            self.grads = grads
            self.near = lax.ppermute(total_of(grads[1], grads[3]), "row", [(r, r ^ 2) for r in range(n_row)])

        def total(self):
            keep, _, got, _ = self.grads
            far = jnp.where(self.even_z, self.near[1], self.near[0])
            mine = jnp.where(self.even_z, self.near[0], self.near[1])
            rest = lax.ppermute(total_of(keep[1], got[1], far), "row", [(r, r ^ 4) for r in range(n_row)])
            return total_of(keep[0], got[0], mine, rest)

    def shards(tokens, out_grad, gate_weight, up_weight, down_weight, gate_rows, up_rows, down_columns):
        f_total, part = gate_weight.shape[:2]
        kg = gate_rows.shape[1]
        row = lax.axis_index("row")
        z, core = row // 2, row % 2
        whole_tiles = part == BS
        slots = list(range(0, nz, 2)) + list(range(1, nz, 2))
        spots = (z - jnp.array(slots, dtype=jnp.int32)) % nz
        order = jnp.concatenate([2 * spots + core, 2 * spots + 1 - core]) if whole_tiles else spots
        scal = jnp.concatenate(
            [t.reshape(-1) for t in (gate_rows, up_rows, down_columns)]
            + [order.astype(jnp.int32), lax.axis_index("col").astype(jnp.int32).reshape(1)]
        )
        pieces = pieces_of(tokens.shape[1] // BS)
        panels = lax.all_gather(jnp.stack([tokens, out_grad]), "col")

        def own_tiles(start, stop):
            return jnp.stack([w[start:stop] for w in (gate_weight, up_weight, down_weight)])

        def all_tiles(mine):
            even, odd = jnp.stack(mine[0::2]), jnp.stack(mine[1::2])
            other_even, other_odd = swap(even), swap(odd)
            if whole_tiles:
                return [even, odd, other_even, other_odd]
            return [
                jnp.where(core == 0, jnp.concatenate([a, b], -2), jnp.concatenate([b, a], -2))
                for a, b in ((even, other_even), (odd, other_odd))
            ]

        def exchanged(tile_grads, hold):
            if whole_tiles:
                keep, give = tile_grads[:2], tile_grads[2:]
            else:
                keep = [lax.dynamic_slice_in_dim(g, core * part, part, 4) for g in tile_grads]
                give = [lax.dynamic_slice_in_dim(g, (1 - core) * part, part, 4) for g in tile_grads]
            give, _ = lax.optimization_barrier((give, hold))
            got_odd = swap(give[1])
            return [keep[0], keep[1], swap(give[0]), got_odd]

        width = tokens.shape[1]

        def compute(f_first, f_here, tiles, tile_first, after=(), hold=()):
            tile_grads, stash = run_grads(
                scal, panels, after, tiles, f_total=f_total, f_first=f_first, f_here=f_here, tile_first=tile_first
            )
            return exchanged(tile_grads, hold), (f_first, stash, tiles, tile_first)

        def add_up(accs, parts, last, after=()):
            return run_adds(scal, accs, after, parts, pieces, n_col=n_col, width=width, f_total=f_total, last=last)

        if f_total % 7 == 0 and f_total > 7 and nz == 4 and whole_tiles:
            few = f_total // 7
            at = [0, few, 3 * few, 4 * few, 6 * few, 7 * few]
            tiles = all_tiles(Chain(z, own_tiles(at[0], at[2])).run(3).slots())
            one, two, three = [Chain(z, own_tiles(at[i], at[i + 1])) for i in (2, 3, 4)]
            one.run(1)
            two.run(1)
            one.grads, part_0 = compute(at[0], few, tiles, at[0], (), one.received(0))
            one.run(1)
            two.grads, part_1 = compute(
                at[1], 2 * few, tiles, at[1], (one.grads[3],), one.received(1) + two.received(0)
            )
            one.tie(1, two.grads[0])
            accs = add_up(None, [part_0, part_1], False)
            one.run(1)
            two.run(1)
            one.tie(2, accs[0])
            mine = one.slots()
            one.run(1)
            two.run(1)
            three.run(1)
            three.grads, part_2 = compute(
                at[2], few, all_tiles(mine), 0, (), three.received(0) + two.received(1)
            )
            three.run(1)
            grads, part_3 = compute(
                at[3], 2 * few, all_tiles(two.slots()), 0, (three.grads[3],), three.received(1) + one.received(3)
            )
            fourth = Halves(z, grads)
            three.run(1)
            mine = three.slots()
            last, part_4 = compute(at[4], few, all_tiles(mine), 0, (grads[3],))
            accs = add_up(accs, [part_2, part_3, part_4], True, (last[3],))
            *accs, _ = lax.optimization_barrier((*accs, fourth.near))
            two.run(1)
            three.run(1)
            sums = [one.total(), two.total(), three.total(), fourth.total(), Halves(z, last).total()]
        else:
            gather = Chain(z, own_tiles(0, f_total)).run(nz - 1)
            grads, part_0 = compute(0, f_total, all_tiles(gather.slots()), 0)
            accs = add_up(None, [part_0], True)
            sums = [Chain(z, None, grads).run(nz - 1).total()]

        output, input_grad = sum_columns(accs)
        weight_grads = [jnp.concatenate([jnp.swapaxes(g[kind], 1, 2) for g in sums], axis=0) for kind in range(3)]
        return (output, input_grad, *weight_grads)

    return shards


def solution(mesh):
    in_specs = (
        P("row", "col"),
        P("row", "col"),
        P("col", "row", None),
        P("col", "row", None),
        P("col", "row", None),
        P("col", None),
        P("col", None),
        P("col", None),
    )
    out_specs = in_specs[:5]
    shards = make_shards(mesh.shape["row"], mesh.shape["col"])
    return jax.shard_map(shards, mesh=mesh, in_specs=in_specs, out_specs=out_specs, check_vma=False)
```

```python
import functools

import jax
import jax.numpy as jnp
from jax import lax
from jax.experimental import pallas as pl
from jax.experimental.pallas import tpu as pltpu
from jax.sharding import PartitionSpec as P

BS = 128
BF = jnp.bfloat16
F32 = jnp.float32


def contract(a, b, da, db):
    return lax.dot_general(a, b, (((da,), (db,)), ((), ())), preferred_element_type=F32)


def taker(refs):
    refs = list(refs)

    def take(count):
        got = refs[:count]
        del refs[:count]
        return got

    return take


def places(scal, table, f, *, kg, f_total, blocks):
    found = []
    for s in range(kg):
        block = scal[table * f_total * kg + f * kg + scal[3 * f_total * kg + s]]
        found.append((block // blocks, lax.rem(block, blocks)))
    return found


def stacked(tiles, kind, j):
    return jnp.concatenate([tile[i, kind, j] for tile in tiles for i in range(tile.shape[0])], axis=0)


def grad_kernel(scal, *refs, n_col, groups, waits, per, kg, f_total, f_first, blocks):
    take = taker(refs)
    (panels,) = take(1)
    take(waits)
    tiles = take(groups)
    tile_grads = take(groups)
    stash, x_all, y_all, load_sem = take(4)
    step = pl.program_id(0)
    both = (x_all, y_all)
    loads = [
        [pltpu.make_async_copy(panels.at[slot, kind], both[kind].at[slot], load_sem.at[kind, slot]) for slot in range(n_col)]
        for kind in range(2)
    ]

    def picked(source, table, j):
        where = places(scal, table, f_first + step * per + j, kg=kg, f_total=f_total, blocks=blocks)
        return jnp.concatenate([source[slot, :, pl.ds(pl.multiple_of(block * BS, BS), BS)] for slot, block in where], axis=1)

    def put(kind, j, grads):
        s = 0
        for ref in tile_grads:
            for i in range(ref.shape[0]):
                ref[i, kind, j] = grads[:, s * BS : (s + 1) * BS].astype(BF)
                s += 1

    def body(before_y):
        fs = range(per)
        x_gate = [picked(x_all, 0, j) for j in fs]
        x_up = [picked(x_all, 1, j) for j in fs]
        gates = [contract(x_gate[j], stacked(tiles, 0, j), 1, 0) for j in fs]
        ups = [contract(x_up[j], stacked(tiles, 1, j), 1, 0) for j in fs]
        before_y()
        y_down = [picked(y_all, 2, j) for j in fs]
        downs = [contract(y_down[j], stacked(tiles, 2, j), 1, 0) for j in fs]
        for j in fs:
            gate, up, hidden_grad = gates[j], ups[j], downs[j]
            sig = jax.nn.sigmoid(gate)
            silu = gate * sig
            hidden = (silu * up).astype(BF)
            gate_grad = (hidden_grad * up * sig * (1.0 + gate * (1.0 - sig))).astype(BF)
            up_grad = (hidden_grad * silu).astype(BF)
            for kind, value, source in ((2, hidden, y_down[j]), (0, gate_grad, x_gate[j]), (1, up_grad, x_up[j])):
                turned = value.T
                stash[kind, j] = turned
                put(kind, j, contract(turned, source, 1, 0))

    @pl.when(step == 0)
    def _():
        for copy in loads[0] + loads[1]:
            copy.start()
        for copy in loads[0]:
            copy.wait()

        def wait_y():
            for copy in loads[1]:
                copy.wait()

        body(wait_y)

    @pl.when(step > 0)
    def _():
        body(lambda: None)


def run_grads(scal, panels, after, tiles, *, f_total, f_first, f_here, tile_first):
    n_col, _, tokens, width = panels.shape
    kg = sum(t.shape[0] for t in tiles)
    per = 2 if f_here % 2 == 0 and tile_first % 2 == 0 else 1
    anywhere = pl.BlockSpec(memory_space=pl.ANY)

    def tile_spec(t, first):
        return pl.BlockSpec((t.shape[0], 3, per, BS, BS), lambda f, scal: (0, 0, f + first, 0, 0))

    kernel = functools.partial(
        grad_kernel,
        n_col=n_col,
        groups=len(tiles),
        waits=len(after),
        per=per,
        kg=kg,
        f_total=f_total,
        f_first=f_first,
        blocks=width // BS,
    )
    out = pl.pallas_call(
        kernel,
        grid_spec=pltpu.PrefetchScalarGridSpec(
            num_scalar_prefetch=1,
            grid=(f_here // per,),
            in_specs=[anywhere] * (1 + len(after)) + [tile_spec(t, tile_first // per) for t in tiles],
            out_specs=[tile_spec(t, 0) for t in tiles]
            + [pl.BlockSpec((3, per, BS, tokens), lambda f, scal: (0, f, 0, 0))],
            scratch_shapes=[
                pltpu.VMEM((n_col, tokens, width), BF),
                pltpu.VMEM((n_col, tokens, width), BF),
                pltpu.SemaphoreType.DMA((2, n_col)),
            ],
        ),
        out_shape=[jax.ShapeDtypeStruct((t.shape[0], 3, f_here, BS, BS), BF) for t in tiles]
        + [jax.ShapeDtypeStruct((3, f_here, BS, tokens), BF)],
        compiler_params=pltpu.CompilerParams(vmem_limit_bytes=48 * 1024 * 1024),
        cost_estimate=pl.CostEstimate(
            flops=6 * 2 * tokens * f_here * kg * BS * BS, bytes_accessed=f_here * 6 * 1024 * 1024, transcendentals=0
        ),
        name="ffn_grads",
    )(scal, panels, *after, *tiles)
    return out[: len(tiles)], out[-1]


def add_kernel(scal, *refs, n_col, pieces, groups, waits, segments, per, kg, f_total, blocks, first, last):
    take = taker(refs)
    take(waits)
    acc_in = [] if first else take(2)
    parts = [(take(1)[0], take(groups)) for _ in segments]
    results = take(len(pieces)) if last else take(2)
    totals = take(2)
    rounded = take(2) if last else []
    acc_sem, store_sem = take(2)
    step = pl.program_id(0)
    me = scal[3 * f_total * kg + kg]
    acc_loads = [pltpu.make_async_copy(src, dst, acc_sem.at[i]) for i, (src, dst) in enumerate(zip(acc_in, totals))]

    def scatter(total, where, tiles_here, turned):
        for (slot, block), tile in zip(where, tiles_here):
            total[(slot ^ me) * blocks + block] += contract(tile, turned, 1, 0)

    @pl.when(step == 0)
    def _():
        for copy in acc_loads:
            copy.start()
        if first:
            for total in totals:
                total[...] = jnp.zeros_like(total)
        for copy in acc_loads:
            copy.wait()

    before = 0
    for (f_first, _, steps), (stash, tiles) in zip(segments, parts):

        @pl.when((step >= before) & (step < before + steps))
        def _():
            for j in range(per):
                f = f_first + (step - before) * per + j
                for kind, total in ((2, totals[0]), (0, totals[1]), (1, totals[1])):
                    where = places(scal, kind, f, kg=kg, f_total=f_total, blocks=blocks)
                    here = [tile[i, kind, j] for tile in tiles for i in range(tile.shape[0])]
                    scatter(total, where, here, stash[kind, j])

        before += steps

    @pl.when(step == before - 1)
    def _():
        stores = []
        for kind, total in enumerate(totals):
            if last:
                for s in range(n_col):
                    for i in range(s * blocks, (s + 1) * blocks):
                        rounded[kind][i] = total[i].astype(BF)
                    here = [
                        pltpu.make_async_copy(
                            rounded[kind].at[pl.ds(slot * blocks + at, count)], results[p].at[kind], store_sem.at[kind, p]
                        )
                        for p, (slot, at, count) in enumerate(pieces)
                        if slot == s
                    ]
                    for copy in here:
                        copy.start()
                    stores += here
            else:
                copy = pltpu.make_async_copy(total, results[kind], acc_sem.at[kind])
                copy.start()
                stores.append(copy)
        for copy in stores:
            copy.wait()


def run_adds(scal, accs, after, parts, pieces, *, n_col, width, f_total, last):
    tokens = parts[0][1].shape[3]
    kg = sum(t.shape[0] for t in parts[0][2])
    first = accs is None
    anywhere = pl.BlockSpec(memory_space=pl.ANY)
    per = 2 if all(stash.shape[1] % 2 == 0 and at % 2 == 0 for _, stash, _, at in parts) else 1
    segments, specs, operands, before = [], [], [], 0
    for f_first, stash, tiles, at in parts:
        steps = stash.shape[1] // per

        def spot(f, before=before, steps=steps):
            return jnp.clip(f - before, 0, steps - 1)

        specs.append(pl.BlockSpec((3, per, BS, tokens), lambda f, scal, spot=spot: (0, spot(f), 0, 0)))
        for t in tiles:
            specs.append(
                pl.BlockSpec(
                    (t.shape[0], 3, per, BS, BS),
                    lambda f, scal, spot=spot, start=at // per: (0, 0, spot(f) + start, 0, 0),
                )
            )
        operands += [stash, *tiles]
        segments.append((f_first, at, steps))
        before += steps
    acc_shape = (n_col * width // BS, BS, tokens)
    if last:
        results = [jax.ShapeDtypeStruct((2, count, BS, tokens), BF) for _, _, count in pieces]
    else:
        results = [jax.ShapeDtypeStruct(acc_shape, F32)] * 2
    kernel = functools.partial(
        add_kernel,
        n_col=n_col,
        pieces=pieces,
        groups=len(parts[0][2]),
        waits=len(after),
        segments=segments,
        per=per,
        kg=kg,
        f_total=f_total,
        blocks=width // BS,
        first=first,
        last=last,
    )
    return pl.pallas_call(
        kernel,
        grid_spec=pltpu.PrefetchScalarGridSpec(
            num_scalar_prefetch=1,
            grid=(before,),
            in_specs=[anywhere] * (len(after) + (0 if first else 2)) + specs,
            out_specs=[anywhere] * len(results),
            scratch_shapes=[pltpu.VMEM(acc_shape, F32)] * 2
            + ([pltpu.VMEM(acc_shape, BF)] * 2 if last else [])
            + [pltpu.SemaphoreType.DMA((2,)), pltpu.SemaphoreType.DMA((2, len(pieces)))],
        ),
        out_shape=results,
        compiler_params=pltpu.CompilerParams(vmem_limit_bytes=56 * 1024 * 1024),
        cost_estimate=pl.CostEstimate(
            flops=3 * 2 * tokens * before * per * kg * BS * BS, bytes_accessed=48 * 1024 * 1024, transcendentals=0
        ),
        name="ffn_adds",
    )(scal, *after, *([] if first else accs), *operands)


def total_of(*terms):
    value = terms[0].astype(F32)
    for term in terms[1:]:
        value = value + term.astype(F32)
    return value.astype(BF)


def make_shards(n_row, n_col):
    nz = n_row // 2
    across = [(r, r ^ 1) for r in range(n_row)]
    two_phase = n_col == 4

    def right(first, stop):
        return [(2 * z + c, 2 * z + 2 + c) for z in range(first, stop) for c in (0, 1)]

    def left(first, stop):
        return [(2 * z + c, 2 * z - 2 + c) for z in range(first, stop) for c in (0, 1)]

    def over(value, offset):
        return lax.ppermute(value, "col", [(i, i ^ offset) for i in range(n_col)])

    def swap(value):
        return lax.ppermute(value, "row", across)

    def pieces_of(blocks):
        half = blocks // 2
        if two_phase:
            return ((0, 0, blocks), (1, 0, blocks), (2, 0, blocks), (3, 0, half), (3, half, blocks - half))
        return tuple((s, 0, blocks) for s in range(n_col))

    def sum_columns(parts, late=()):
        if two_phase:
            mine, beside, above, low, high = parts
            half = low.shape[1]
            low, high = over(low, 1), over(high, 2)
            above = jnp.concatenate([total_of(above[:, :half], low), above[:, half:]], axis=1)
            beside = jnp.concatenate([beside[:, :half], total_of(beside[:, half:], high)], axis=1)
            beside, above, _ = lax.optimization_barrier((beside, above, late))
            got = [over(beside, 1), over(above, 2)]
        else:
            mine = parts[0]
            got = [over(parts[o], o) for o in range(1, n_col)]
        sums = [total_of(mine[i], *[g[i] for g in got]) for i in range(2)]
        return [total.reshape(-1, total.shape[-1]).T for total in sums]

    class Chain:
        paired = nz == 4

        def __init__(self, z, own=None, grads=None):
            self.z, self.own, self.grads = z, own, grads
            self.raw = []
            self.tick = 0 if own is not None else 1

        def part(self, slot):
            return [g[slot // 2] for g in self.grads[slot % 2 :: 2]]

        def from_left(self, i):
            first, second = self.raw[i]
            if not self.paired:
                return first
            zero = jnp.zeros((), first.dtype)
            return jnp.where(self.z % 2 == 1, first, jnp.where(self.z == 2, second, zero))

        def from_right(self, i):
            first, second = self.raw[i]
            if not self.paired:
                return second
            zero = jnp.zeros((), first.dtype)
            return jnp.where(self.z % 2 == 0, first, jnp.where(self.z == 1, second, zero))

        def run(self, count):
            for _ in range(count):
                i = self.tick
                summing = self.grads is not None
                if i == 0:
                    to_right = to_left = self.own
                elif not summing:
                    to_right, to_left = self.from_left(-1), self.from_right(-1)
                else:
                    came = bool(self.raw)
                    to_right = total_of(*self.part(i), *([self.from_left(-1)] if came else []))
                    to_left = total_of(*self.part(nz - i), *([self.from_right(-1)] if came else []))
                    if self.own is not None:
                        to_right = jnp.where(self.z >= i, self.from_left(-1), to_right)
                        to_left = jnp.where(nz - 1 - self.z >= i, self.from_right(-1), to_left)
                if self.paired:
                    if i == 0:
                        first = second = self.own
                    elif not summing:
                        second, first = self.raw[-1]
                    else:
                        first = jnp.where(self.z % 2 == 0, to_right, to_left)
                        second = jnp.where(self.z == 1, to_right, to_left)
                    middle = [(r, r) if r // 2 in (0, 3) else (r, r ^ 6) for r in range(n_row)]
                    self.raw.append(
                        (
                            lax.ppermute(first, "row", [(r, r ^ 2) for r in range(n_row)]),
                            lax.ppermute(second, "row", middle),
                        )
                    )
                else:
                    start = 0 if summing else i
                    stop = nz - 1 if self.own is not None else i
                    self.raw.append(
                        (
                            lax.ppermute(to_right, "row", right(start, stop)),
                            lax.ppermute(to_left, "row", left(nz - stop, nz - start)),
                        )
                    )
                self.tick += 1
            return self

        def received(self, i):
            return self.raw[i]

        def tie(self, i, other):
            *came, _ = lax.optimization_barrier((*self.raw[i], other))
            self.raw[i] = tuple(came)

        def slots(self):
            found = [self.own]
            for o in range(1, nz):
                found.append(jnp.where(self.z >= o, self.from_left(o - 1), self.from_right(nz - o - 1)))
            return found

        def total(self):
            return total_of(*self.part(0), self.from_left(-1), self.from_right(-1))

    class Halves:
        def __init__(self, z, grads):
            self.even_z = z % 2 == 0
            self.grads = grads
            self.near = lax.ppermute(total_of(grads[1], grads[3]), "row", [(r, r ^ 2) for r in range(n_row)])

        def total(self):
            keep, _, got, _ = self.grads
            far = jnp.where(self.even_z, self.near[1], self.near[0])
            mine = jnp.where(self.even_z, self.near[0], self.near[1])
            rest = lax.ppermute(total_of(keep[1], got[1], far), "row", [(r, r ^ 4) for r in range(n_row)])
            return total_of(keep[0], got[0], mine, rest)

    def shards(tokens, out_grad, gate_weight, up_weight, down_weight, gate_rows, up_rows, down_columns):
        f_total, part = gate_weight.shape[:2]
        kg = gate_rows.shape[1]
        row = lax.axis_index("row")
        z, core = row // 2, row % 2
        whole_tiles = part == BS
        slots = list(range(0, nz, 2)) + list(range(1, nz, 2))
        spots = (z - jnp.array(slots, dtype=jnp.int32)) % nz
        order = jnp.concatenate([2 * spots + core, 2 * spots + 1 - core]) if whole_tiles else spots
        scal = jnp.concatenate(
            [t.reshape(-1) for t in (gate_rows, up_rows, down_columns)]
            + [order.astype(jnp.int32), lax.axis_index("col").astype(jnp.int32).reshape(1)]
        )
        pieces = pieces_of(tokens.shape[1] // BS)
        panels = lax.all_gather(jnp.stack([tokens, out_grad]), "col")

        def own_tiles(start, stop):
            return jnp.stack([w[start:stop] for w in (gate_weight, up_weight, down_weight)])

        def all_tiles(mine):
            even, odd = jnp.stack(mine[0::2]), jnp.stack(mine[1::2])
            other_even, other_odd = swap(even), swap(odd)
            if whole_tiles:
                return [even, odd, other_even, other_odd]
            return [
                jnp.where(core == 0, jnp.concatenate([a, b], -2), jnp.concatenate([b, a], -2))
                for a, b in ((even, other_even), (odd, other_odd))
            ]

        def exchanged(tile_grads, hold):
            if whole_tiles:
                keep, give = tile_grads[:2], tile_grads[2:]
            else:
                keep = [lax.dynamic_slice_in_dim(g, core * part, part, 4) for g in tile_grads]
                give = [lax.dynamic_slice_in_dim(g, (1 - core) * part, part, 4) for g in tile_grads]
            give, _ = lax.optimization_barrier((give, hold))
            got_odd = swap(give[1])
            return [keep[0], keep[1], swap(give[0]), got_odd]

        width = tokens.shape[1]

        def compute(f_first, f_here, tiles, tile_first, after=(), hold=()):
            tile_grads, stash = run_grads(
                scal, panels, after, tiles, f_total=f_total, f_first=f_first, f_here=f_here, tile_first=tile_first
            )
            return exchanged(tile_grads, hold), (f_first, stash, tiles, tile_first)

        def add_up(accs, parts, last, after=()):
            return run_adds(scal, accs, after, parts, pieces, n_col=n_col, width=width, f_total=f_total, last=last)

        if f_total % 7 == 0 and f_total > 7 and nz == 4 and whole_tiles:
            few = f_total // 7
            at = [0, few, 3 * few, 4 * few, 6 * few, 7 * few]
            tiles = all_tiles(Chain(z, own_tiles(at[0], at[2])).run(3).slots())
            one, two, three = [Chain(z, own_tiles(at[i], at[i + 1])) for i in (2, 3, 4)]
            one.run(1)
            two.run(1)
            one.grads, part_0 = compute(at[0], few, tiles, at[0], (), one.received(0))
            one.run(1)
            two.grads, part_1 = compute(
                at[1], 2 * few, tiles, at[1], (one.grads[3],), one.received(1) + two.received(0)
            )
            one.tie(1, two.grads[0])
            accs = add_up(None, [part_0, part_1], False)
            one.run(1)
            two.run(1)
            one.tie(2, accs[0])
            mine = one.slots()
            one.run(1)
            two.run(1)
            three.run(1)
            three.grads, part_2 = compute(
                at[2], few, all_tiles(mine), 0, (), three.received(0) + two.received(1)
            )
            three.run(1)
            grads, part_3 = compute(
                at[3], 2 * few, all_tiles(two.slots()), 0, (three.grads[3],), three.received(1) + one.received(3)
            )
            fourth = Halves(z, grads)
            three.run(1)
            mine = three.slots()
            two.run(1)
            last, part_4 = compute(at[4], few, all_tiles(mine), 0, (grads[3],))
            fifth = Halves(z, last)
            three.run(1)
            accs = add_up(accs, [part_2, part_3, part_4], True, (last[3],))
            *accs, _ = lax.optimization_barrier((*accs, (fourth.near, two.received(3))))
            late = (fifth.near, three.received(3))
            sums = [one.total(), two.total(), three.total(), fourth.total(), fifth.total()]
        else:
            gather = Chain(z, own_tiles(0, f_total)).run(nz - 1)
            grads, part_0 = compute(0, f_total, all_tiles(gather.slots()), 0)
            accs = add_up(None, [part_0], True)
            late = ()
            sums = [Chain(z, None, grads).run(nz - 1).total()]

        output, input_grad = sum_columns(accs, late)
        weight_grads = [jnp.concatenate([jnp.swapaxes(g[kind], 1, 2) for g in sums], axis=0) for kind in range(3)]
        return (output, input_grad, *weight_grads)

    return shards


def solution(mesh):
    in_specs = (
        P("row", "col"),
        P("row", "col"),
        P("col", "row", None),
        P("col", "row", None),
        P("col", "row", None),
        P("col", None),
        P("col", None),
        P("col", None),
    )
    out_specs = in_specs[:5]
    shards = make_shards(mesh.shape["row"], mesh.shape["col"])
    return jax.shard_map(shards, mesh=mesh, in_specs=in_specs, out_specs=out_specs, check_vma=False)
```

```python
import functools

import jax
import jax.numpy as jnp
from jax import lax
from jax.experimental import pallas as pl
from jax.experimental.pallas import tpu as pltpu
from jax.sharding import PartitionSpec as P

BS = 128
BF = jnp.bfloat16
F32 = jnp.float32


def contract(a, b, da, db):
    return lax.dot_general(a, b, (((da,), (db,)), ((), ())), preferred_element_type=F32)


def taker(refs):
    refs = list(refs)

    def take(count):
        got = refs[:count]
        del refs[:count]
        return got

    return take


def places(scal, table, f, *, kg, f_total, blocks):
    found = []
    for s in range(kg):
        block = scal[table * f_total * kg + f * kg + scal[3 * f_total * kg + s]]
        found.append((block // blocks, lax.rem(block, blocks)))
    return found


def stacked(tiles, kind, j):
    return jnp.concatenate([tile[i, kind, j] for tile in tiles for i in range(tile.shape[0])], axis=0)


def grad_kernel(scal, *refs, n_col, groups, waits, per, kg, f_total, f_first, blocks):
    take = taker(refs)
    (panels,) = take(1)
    take(waits)
    tiles = take(groups)
    tile_grads = take(groups)
    stash, x_all, y_all, load_sem = take(4)
    step = pl.program_id(0)
    both = (x_all, y_all)
    loads = [
        [pltpu.make_async_copy(panels.at[slot, kind], both[kind].at[slot], load_sem.at[kind, slot]) for slot in range(n_col)]
        for kind in range(2)
    ]

    def picked(source, table, j):
        where = places(scal, table, f_first + step * per + j, kg=kg, f_total=f_total, blocks=blocks)
        return jnp.concatenate([source[slot, :, pl.ds(pl.multiple_of(block * BS, BS), BS)] for slot, block in where], axis=1)

    def put(kind, j, grads):
        s = 0
        for ref in tile_grads:
            for i in range(ref.shape[0]):
                ref[i, kind, j] = grads[:, s * BS : (s + 1) * BS].astype(BF)
                s += 1

    def body(before_y):
        fs = range(per)
        x_gate = [picked(x_all, 0, j) for j in fs]
        x_up = [picked(x_all, 1, j) for j in fs]
        gates = [contract(x_gate[j], stacked(tiles, 0, j), 1, 0) for j in fs]
        ups = [contract(x_up[j], stacked(tiles, 1, j), 1, 0) for j in fs]
        before_y()
        y_down = [picked(y_all, 2, j) for j in fs]
        downs = [contract(y_down[j], stacked(tiles, 2, j), 1, 0) for j in fs]
        for j in fs:
            gate, up, hidden_grad = gates[j], ups[j], downs[j]
            sig = jax.nn.sigmoid(gate)
            silu = gate * sig
            hidden = (silu * up).astype(BF)
            gate_grad = (hidden_grad * up * sig * (1.0 + gate * (1.0 - sig))).astype(BF)
            up_grad = (hidden_grad * silu).astype(BF)
            for kind, value, source in ((2, hidden, y_down[j]), (0, gate_grad, x_gate[j]), (1, up_grad, x_up[j])):
                turned = value.T
                stash[kind, j] = turned
                put(kind, j, contract(turned, source, 1, 0))

    @pl.when(step == 0)
    def _():
        for copy in loads[0] + loads[1]:
            copy.start()
        for copy in loads[0]:
            copy.wait()

        def wait_y():
            for copy in loads[1]:
                copy.wait()

        body(wait_y)

    @pl.when(step > 0)
    def _():
        body(lambda: None)


def run_grads(scal, panels, after, tiles, *, f_total, f_first, f_here, tile_first):
    n_col, _, tokens, width = panels.shape
    kg = sum(t.shape[0] for t in tiles)
    per = 2 if f_here % 2 == 0 and tile_first % 2 == 0 else 1
    anywhere = pl.BlockSpec(memory_space=pl.ANY)

    def tile_spec(t, first):
        return pl.BlockSpec((t.shape[0], 3, per, BS, BS), lambda f, scal: (0, 0, f + first, 0, 0))

    kernel = functools.partial(
        grad_kernel,
        n_col=n_col,
        groups=len(tiles),
        waits=len(after),
        per=per,
        kg=kg,
        f_total=f_total,
        f_first=f_first,
        blocks=width // BS,
    )
    out = pl.pallas_call(
        kernel,
        grid_spec=pltpu.PrefetchScalarGridSpec(
            num_scalar_prefetch=1,
            grid=(f_here // per,),
            in_specs=[anywhere] * (1 + len(after)) + [tile_spec(t, tile_first // per) for t in tiles],
            out_specs=[tile_spec(t, 0) for t in tiles]
            + [pl.BlockSpec((3, per, BS, tokens), lambda f, scal: (0, f, 0, 0))],
            scratch_shapes=[
                pltpu.VMEM((n_col, tokens, width), BF),
                pltpu.VMEM((n_col, tokens, width), BF),
                pltpu.SemaphoreType.DMA((2, n_col)),
            ],
        ),
        out_shape=[jax.ShapeDtypeStruct((t.shape[0], 3, f_here, BS, BS), BF) for t in tiles]
        + [jax.ShapeDtypeStruct((3, f_here, BS, tokens), BF)],
        compiler_params=pltpu.CompilerParams(vmem_limit_bytes=48 * 1024 * 1024),
        cost_estimate=pl.CostEstimate(
            flops=6 * 2 * tokens * f_here * kg * BS * BS, bytes_accessed=f_here * 6 * 1024 * 1024, transcendentals=0
        ),
        name="ffn_grads",
    )(scal, panels, *after, *tiles)
    return out[: len(tiles)], out[-1]


def add_kernel(scal, *refs, n_col, pieces, groups, waits, segments, per, kg, f_total, blocks, first, last):
    take = taker(refs)
    take(waits)
    acc_in = [] if first else take(2)
    parts = [(take(1)[0], take(groups)) for _ in segments]
    results = take(len(pieces)) if last else take(2)
    totals = take(2)
    rounded = take(2) if last else []
    acc_sem, store_sem = take(2)
    step = pl.program_id(0)
    me = scal[3 * f_total * kg + kg]
    acc_loads = [pltpu.make_async_copy(src, dst, acc_sem.at[i]) for i, (src, dst) in enumerate(zip(acc_in, totals))]

    def scatter(total, where, tile_rows, turned):
        added = contract(tile_rows, turned, 1, 0)
        for s, (slot, block) in enumerate(where):
            total[(slot ^ me) * blocks + block] += added[s * BS : (s + 1) * BS]

    @pl.when(step == 0)
    def _():
        for copy in acc_loads:
            copy.start()
        if first:
            for total in totals:
                total[...] = jnp.zeros_like(total)
        for copy in acc_loads:
            copy.wait()

    before = 0
    for (f_first, _, steps), (stash, tiles) in zip(segments, parts):

        @pl.when((step >= before) & (step < before + steps))
        def _():
            for j in range(per):
                f = f_first + (step - before) * per + j
                for kind, total in ((2, totals[0]), (0, totals[1]), (1, totals[1])):
                    where = places(scal, kind, f, kg=kg, f_total=f_total, blocks=blocks)
                    scatter(total, where, stacked(tiles, kind, j), stash[kind, j])

        before += steps

    @pl.when(step == before - 1)
    def _():
        stores = []
        for kind, total in enumerate(totals):
            if last:
                for s in range(n_col):
                    for i in range(s * blocks, (s + 1) * blocks):
                        rounded[kind][i] = total[i].astype(BF)
                    here = [
                        pltpu.make_async_copy(
                            rounded[kind].at[pl.ds(slot * blocks + at, count)], results[p].at[kind], store_sem.at[kind, p]
                        )
                        for p, (slot, at, count) in enumerate(pieces)
                        if slot == s
                    ]
                    for copy in here:
                        copy.start()
                    stores += here
            else:
                copy = pltpu.make_async_copy(total, results[kind], acc_sem.at[kind])
                copy.start()
                stores.append(copy)
        for copy in stores:
            copy.wait()


def run_adds(scal, accs, after, parts, pieces, *, n_col, width, f_total, last):
    tokens = parts[0][1].shape[3]
    kg = sum(t.shape[0] for t in parts[0][2])
    first = accs is None
    anywhere = pl.BlockSpec(memory_space=pl.ANY)
    per = 2 if all(stash.shape[1] % 2 == 0 and at % 2 == 0 for _, stash, _, at in parts) else 1
    segments, specs, operands, before = [], [], [], 0
    for f_first, stash, tiles, at in parts:
        steps = stash.shape[1] // per

        def spot(f, before=before, steps=steps):
            return jnp.clip(f - before, 0, steps - 1)

        specs.append(pl.BlockSpec((3, per, BS, tokens), lambda f, scal, spot=spot: (0, spot(f), 0, 0)))
        for t in tiles:
            specs.append(
                pl.BlockSpec(
                    (t.shape[0], 3, per, BS, BS),
                    lambda f, scal, spot=spot, start=at // per: (0, 0, spot(f) + start, 0, 0),
                )
            )
        operands += [stash, *tiles]
        segments.append((f_first, at, steps))
        before += steps
    acc_shape = (n_col * width // BS, BS, tokens)
    if last:
        results = [jax.ShapeDtypeStruct((2, count, BS, tokens), BF) for _, _, count in pieces]
    else:
        results = [jax.ShapeDtypeStruct(acc_shape, F32)] * 2
    kernel = functools.partial(
        add_kernel,
        n_col=n_col,
        pieces=pieces,
        groups=len(parts[0][2]),
        waits=len(after),
        segments=segments,
        per=per,
        kg=kg,
        f_total=f_total,
        blocks=width // BS,
        first=first,
        last=last,
    )
    return pl.pallas_call(
        kernel,
        grid_spec=pltpu.PrefetchScalarGridSpec(
            num_scalar_prefetch=1,
            grid=(before,),
            in_specs=[anywhere] * (len(after) + (0 if first else 2)) + specs,
            out_specs=[anywhere] * len(results),
            scratch_shapes=[pltpu.VMEM(acc_shape, F32)] * 2
            + ([pltpu.VMEM(acc_shape, BF)] * 2 if last else [])
            + [pltpu.SemaphoreType.DMA((2,)), pltpu.SemaphoreType.DMA((2, len(pieces)))],
        ),
        out_shape=results,
        compiler_params=pltpu.CompilerParams(vmem_limit_bytes=56 * 1024 * 1024),
        cost_estimate=pl.CostEstimate(
            flops=3 * 2 * tokens * before * per * kg * BS * BS, bytes_accessed=48 * 1024 * 1024, transcendentals=0
        ),
        name="ffn_adds",
    )(scal, *after, *([] if first else accs), *operands)


def total_of(*terms):
    value = terms[0].astype(F32)
    for term in terms[1:]:
        value = value + term.astype(F32)
    return value.astype(BF)


def make_shards(n_row, n_col):
    nz = n_row // 2
    across = [(r, r ^ 1) for r in range(n_row)]
    two_phase = n_col == 4

    def right(first, stop):
        return [(2 * z + c, 2 * z + 2 + c) for z in range(first, stop) for c in (0, 1)]

    def left(first, stop):
        return [(2 * z + c, 2 * z - 2 + c) for z in range(first, stop) for c in (0, 1)]

    def over(value, offset):
        return lax.ppermute(value, "col", [(i, i ^ offset) for i in range(n_col)])

    def swap(value):
        return lax.ppermute(value, "row", across)

    def pieces_of(blocks):
        half = blocks // 2
        if two_phase:
            return ((0, 0, blocks), (1, 0, blocks), (2, 0, blocks), (3, 0, half), (3, half, blocks - half))
        return tuple((s, 0, blocks) for s in range(n_col))

    def sum_columns(parts):
        if two_phase:
            mine, beside, above, low, high = parts
            half = low.shape[1]
            low, high = over(low, 1), over(high, 2)
            above = jnp.concatenate([total_of(above[:, :half], low), above[:, half:]], axis=1)
            beside = jnp.concatenate([beside[:, :half], total_of(beside[:, half:], high)], axis=1)
            got = [over(beside, 1), over(above, 2)]
        else:
            mine = parts[0]
            got = [over(parts[o], o) for o in range(1, n_col)]
        sums = [total_of(mine[i], *[g[i] for g in got]) for i in range(2)]
        return [total.reshape(-1, total.shape[-1]).T for total in sums]

    class Chain:
        def __init__(self, z, own=None, grads=None):
            self.z, self.own, self.grads = z, own, grads
            self.from_left, self.from_right = [], []
            self.tick = 0 if own is not None else 1

        def part(self, slot):
            return [g[slot // 2] for g in self.grads[slot % 2 :: 2]]

        def run(self, count):
            for _ in range(count):
                i = self.tick
                summing = self.grads is not None
                if i == 0:
                    to_right = to_left = self.own
                elif not summing:
                    to_right, to_left = self.from_left[-1], self.from_right[-1]
                else:
                    to_right = total_of(*self.part(i), *self.from_left[-1:])
                    to_left = total_of(*self.part(nz - i), *self.from_right[-1:])
                    if self.own is not None:
                        to_right = jnp.where(self.z >= i, self.from_left[-1], to_right)
                        to_left = jnp.where(nz - 1 - self.z >= i, self.from_right[-1], to_left)
                start = 0 if summing else i
                stop = nz - 1 if self.own is not None else i
                self.from_left.append(lax.ppermute(to_right, "row", right(start, stop)))
                self.from_right.append(lax.ppermute(to_left, "row", left(nz - stop, nz - start)))
                self.tick += 1
            return self

        def received(self, i):
            return (self.from_left[i], self.from_right[i])

        def tie(self, i, other):
            self.from_left[i], self.from_right[i], _ = lax.optimization_barrier((*self.received(i), other))

        def slots(self):
            found = [self.own]
            for o in range(1, nz):
                found.append(jnp.where(self.z >= o, self.from_left[o - 1], self.from_right[nz - o - 1]))
            return found

        def total(self):
            return total_of(*self.part(0), self.from_left[-1], self.from_right[-1])

    class Halves:
        def __init__(self, z, grads):
            self.even_z = z % 2 == 0
            self.grads = grads
            self.near = lax.ppermute(total_of(grads[1], grads[3]), "row", [(r, r ^ 2) for r in range(n_row)])

        def finish(self, after=()):
            keep, _, got, _ = self.grads
            near, _ = lax.optimization_barrier((self.near, after))
            far = jnp.where(self.even_z, near[1], near[0])
            self.mine = jnp.where(self.even_z, near[0], near[1])
            self.rest = lax.ppermute(total_of(keep[1], got[1], far), "row", [(r, r ^ 4) for r in range(n_row)])
            return self

        def total(self):
            keep, _, got, _ = self.grads
            return total_of(keep[0], got[0], self.mine, self.rest)

    def shards(tokens, out_grad, gate_weight, up_weight, down_weight, gate_rows, up_rows, down_columns):
        f_total, part = gate_weight.shape[:2]
        kg = gate_rows.shape[1]
        row = lax.axis_index("row")
        z, core = row // 2, row % 2
        whole_tiles = part == BS
        slots = list(range(0, nz, 2)) + list(range(1, nz, 2))
        spots = (z - jnp.array(slots, dtype=jnp.int32)) % nz
        order = jnp.concatenate([2 * spots + core, 2 * spots + 1 - core]) if whole_tiles else spots
        scal = jnp.concatenate(
            [t.reshape(-1) for t in (gate_rows, up_rows, down_columns)]
            + [order.astype(jnp.int32), lax.axis_index("col").astype(jnp.int32).reshape(1)]
        )
        pieces = pieces_of(tokens.shape[1] // BS)
        panels = lax.all_gather(jnp.stack([tokens, out_grad]), "col")

        def own_tiles(start, stop):
            return jnp.stack([w[start:stop] for w in (gate_weight, up_weight, down_weight)])

        def all_tiles(mine):
            even, odd = jnp.stack(mine[0::2]), jnp.stack(mine[1::2])
            other_even, other_odd = swap(even), swap(odd)
            if whole_tiles:
                return [even, odd, other_even, other_odd]
            return [
                jnp.where(core == 0, jnp.concatenate([a, b], -2), jnp.concatenate([b, a], -2))
                for a, b in ((even, other_even), (odd, other_odd))
            ]

        def exchanged(tile_grads, hold):
            if whole_tiles:
                keep, give = tile_grads[:2], tile_grads[2:]
            else:
                keep = [lax.dynamic_slice_in_dim(g, core * part, part, 4) for g in tile_grads]
                give = [lax.dynamic_slice_in_dim(g, (1 - core) * part, part, 4) for g in tile_grads]
            give, _ = lax.optimization_barrier((give, hold))
            got_odd = swap(give[1])
            return [keep[0], keep[1], swap(give[0]), got_odd]

        width = tokens.shape[1]

        def compute(f_first, f_here, tiles, tile_first, after=(), hold=()):
            tile_grads, stash = run_grads(
                scal, panels, after, tiles, f_total=f_total, f_first=f_first, f_here=f_here, tile_first=tile_first
            )
            return exchanged(tile_grads, hold), (f_first, stash, tiles, tile_first)

        def add_up(accs, parts, last, after=()):
            return run_adds(scal, accs, after, parts, pieces, n_col=n_col, width=width, f_total=f_total, last=last)

        if f_total % 7 == 0 and f_total > 7 and nz == 4 and whole_tiles:
            few = f_total // 7
            at = [0, few, 3 * few, 4 * few, 6 * few, 7 * few]
            tiles = all_tiles(Chain(z, own_tiles(at[0], at[2])).run(3).slots())
            one, two, three = [Chain(z, own_tiles(at[i], at[i + 1])) for i in (2, 3, 4)]
            one.run(1)
            two.run(1)
            one.grads, part_0 = compute(at[0], few, tiles, at[0], (), one.received(0))
            one.run(1)
            two.grads, part_1 = compute(
                at[1], 2 * few, tiles, at[1], (one.grads[3],), one.received(1) + two.received(0)
            )
            one.tie(1, two.grads[0])
            accs = add_up(None, [part_0, part_1], False)
            one.run(1)
            two.run(1)
            one.tie(2, accs[0])
            mine = one.slots()
            one.run(1)
            two.run(1)
            three.run(1)
            three.grads, part_2 = compute(
                at[2], few, all_tiles(mine), 0, (), three.received(0) + two.received(1)
            )
            three.run(1)
            grads, part_3 = compute(
                at[3], 2 * few, all_tiles(two.slots()), 0, (three.grads[3],), three.received(1) + one.received(3)
            )
            fourth = Halves(z, grads)
            three.run(1)
            mine = three.slots()
            last, part_4 = compute(at[4], few, all_tiles(mine), 0, (grads[3],))
            accs = add_up(accs, [part_2, part_3, part_4], True, (last[3],))
            *accs, _ = lax.optimization_barrier((*accs, fourth.near))
            two.run(1)
            three.run(1)
            fifth = Halves(z, last)
            fourth.finish()
            fifth.finish((fourth.rest,))
            sums = [one.total(), two.total(), three.total(), fourth.total(), fifth.total()]
        else:
            gather = Chain(z, own_tiles(0, f_total)).run(nz - 1)
            grads, part_0 = compute(0, f_total, all_tiles(gather.slots()), 0)
            accs = add_up(None, [part_0], True)
            sums = [Chain(z, None, grads).run(nz - 1).total()]

        output, input_grad = sum_columns(accs)
        weight_grads = [jnp.concatenate([jnp.swapaxes(g[kind], 1, 2) for g in sums], axis=0) for kind in range(3)]
        return (output, input_grad, *weight_grads)

    return shards


def solution(mesh):
    in_specs = (
        P("row", "col"),
        P("row", "col"),
        P("col", "row", None),
        P("col", "row", None),
        P("col", "row", None),
        P("col", None),
        P("col", None),
        P("col", None),
    )
    out_specs = in_specs[:5]
    shards = make_shards(mesh.shape["row"], mesh.shape["col"])
    return jax.shard_map(shards, mesh=mesh, in_specs=in_specs, out_specs=out_specs, check_vma=False)
```

```python
import functools

import jax
import jax.numpy as jnp
from jax import lax
from jax.experimental import pallas as pl
from jax.experimental.pallas import tpu as pltpu
from jax.sharding import PartitionSpec as P

BS = 128
BF = jnp.bfloat16
F32 = jnp.float32


def contract(a, b, da, db):
    return lax.dot_general(a, b, (((da,), (db,)), ((), ())), preferred_element_type=F32)


def taker(refs):
    refs = list(refs)

    def take(count):
        got = refs[:count]
        del refs[:count]
        return got

    return take


def places(scal, table, f, *, kg, f_total, blocks):
    found = []
    for s in range(kg):
        block = scal[table * f_total * kg + f * kg + scal[3 * f_total * kg + s]]
        found.append((block // blocks, lax.rem(block, blocks)))
    return found


def stacked(tiles, kind, j):
    return jnp.concatenate([tile[i, kind, j] for tile in tiles for i in range(tile.shape[0])], axis=0)


def grad_kernel(scal, *refs, n_col, groups, waits, per, kg, f_total, f_first, blocks):
    take = taker(refs)
    (panels,) = take(1)
    take(waits)
    tiles = take(groups)
    tile_grads = take(groups)
    stash, x_all, y_all, load_sem = take(4)
    step = pl.program_id(0)
    both = (x_all, y_all)
    loads = [
        [pltpu.make_async_copy(panels.at[slot, kind], both[kind].at[slot], load_sem.at[kind, slot]) for slot in range(n_col)]
        for kind in range(2)
    ]

    def picked(source, table, j):
        where = places(scal, table, f_first + step * per + j, kg=kg, f_total=f_total, blocks=blocks)
        return jnp.concatenate([source[slot, :, pl.ds(pl.multiple_of(block * BS, BS), BS)] for slot, block in where], axis=1)

    def put(kind, j, grads):
        s = 0
        for ref in tile_grads:
            for i in range(ref.shape[0]):
                ref[i, kind, j] = grads[:, s * BS : (s + 1) * BS].astype(BF)
                s += 1

    def body(before_y):
        fs = range(per)
        x_gate = [picked(x_all, 0, j) for j in fs]
        x_up = [picked(x_all, 1, j) for j in fs]
        gates = [contract(x_gate[j], stacked(tiles, 0, j), 1, 0) for j in fs]
        ups = [contract(x_up[j], stacked(tiles, 1, j), 1, 0) for j in fs]
        before_y()
        y_down = [picked(y_all, 2, j) for j in fs]
        downs = [contract(y_down[j], stacked(tiles, 2, j), 1, 0) for j in fs]
        for j in fs:
            gate, up, hidden_grad = gates[j], ups[j], downs[j]
            sig = jax.nn.sigmoid(gate)
            silu = gate * sig
            hidden = (silu * up).astype(BF)
            gate_grad = (hidden_grad * up * sig * (1.0 + gate * (1.0 - sig))).astype(BF)
            up_grad = (hidden_grad * silu).astype(BF)
            for kind, value, source in ((2, hidden, y_down[j]), (0, gate_grad, x_gate[j]), (1, up_grad, x_up[j])):
                turned = value.T
                stash[kind, j] = turned
                put(kind, j, contract(turned, source, 1, 0))

    @pl.when(step == 0)
    def _():
        for copy in loads[0] + loads[1]:
            copy.start()
        for copy in loads[0]:
            copy.wait()

        def wait_y():
            for copy in loads[1]:
                copy.wait()

        body(wait_y)

    @pl.when(step > 0)
    def _():
        body(lambda: None)


def run_grads(scal, panels, after, tiles, *, f_total, f_first, f_here, tile_first):
    n_col, _, tokens, width = panels.shape
    kg = sum(t.shape[0] for t in tiles)
    per = 2 if f_here % 2 == 0 and tile_first % 2 == 0 else 1
    anywhere = pl.BlockSpec(memory_space=pl.ANY)

    def tile_spec(t, first):
        return pl.BlockSpec((t.shape[0], 3, per, BS, BS), lambda f, scal: (0, 0, f + first, 0, 0))

    kernel = functools.partial(
        grad_kernel,
        n_col=n_col,
        groups=len(tiles),
        waits=len(after),
        per=per,
        kg=kg,
        f_total=f_total,
        f_first=f_first,
        blocks=width // BS,
    )
    out = pl.pallas_call(
        kernel,
        grid_spec=pltpu.PrefetchScalarGridSpec(
            num_scalar_prefetch=1,
            grid=(f_here // per,),
            in_specs=[anywhere] * (1 + len(after)) + [tile_spec(t, tile_first // per) for t in tiles],
            out_specs=[tile_spec(t, 0) for t in tiles]
            + [pl.BlockSpec((3, per, BS, tokens), lambda f, scal: (0, f, 0, 0))],
            scratch_shapes=[
                pltpu.VMEM((n_col, tokens, width), BF),
                pltpu.VMEM((n_col, tokens, width), BF),
                pltpu.SemaphoreType.DMA((2, n_col)),
            ],
        ),
        out_shape=[jax.ShapeDtypeStruct((t.shape[0], 3, f_here, BS, BS), BF) for t in tiles]
        + [jax.ShapeDtypeStruct((3, f_here, BS, tokens), BF)],
        compiler_params=pltpu.CompilerParams(vmem_limit_bytes=48 * 1024 * 1024),
        cost_estimate=pl.CostEstimate(
            flops=6 * 2 * tokens * f_here * kg * BS * BS, bytes_accessed=f_here * 6 * 1024 * 1024, transcendentals=0
        ),
        name="ffn_grads",
    )(scal, panels, *after, *tiles)
    return out[: len(tiles)], out[-1]


def add_kernel(scal, *refs, n_col, pieces, groups, waits, segments, per, kg, f_total, blocks, first, last):
    take = taker(refs)
    take(waits)
    acc_in = [] if first else take(2)
    parts = [(take(1)[0], take(groups)) for _ in segments]
    results = take(len(pieces)) if last else take(2)
    totals = take(2)
    rounded = take(2) if last else []
    acc_sem, store_sem = take(2)
    step = pl.program_id(0)
    me = scal[3 * f_total * kg + kg]
    acc_loads = [pltpu.make_async_copy(src, dst, acc_sem.at[i]) for i, (src, dst) in enumerate(zip(acc_in, totals))]

    def scatter(total, where, tile_rows, turned):
        added = contract(tile_rows, turned, 1, 0)
        for s, (slot, block) in enumerate(where):
            total[(slot ^ me) * blocks + block] += added[s * BS : (s + 1) * BS]

    @pl.when(step == 0)
    def _():
        for copy in acc_loads:
            copy.start()
        if first:
            for total in totals:
                total[...] = jnp.zeros_like(total)
        for copy in acc_loads:
            copy.wait()

    before = 0
    for (f_first, _, steps), (stash, tiles) in zip(segments, parts):

        @pl.when((step >= before) & (step < before + steps))
        def _():
            for j in range(per):
                f = f_first + (step - before) * per + j
                for kind, total in ((2, totals[0]), (0, totals[1]), (1, totals[1])):
                    where = places(scal, kind, f, kg=kg, f_total=f_total, blocks=blocks)
                    scatter(total, where, stacked(tiles, kind, j), stash[kind, j])

        before += steps

    @pl.when(step == before - 1)
    def _():
        stores = []
        for kind, total in enumerate(totals):
            if last:
                for s in range(n_col):
                    for i in range(s * blocks, (s + 1) * blocks):
                        rounded[kind][i] = total[i].astype(BF)
                    here = [
                        pltpu.make_async_copy(
                            rounded[kind].at[pl.ds(slot * blocks + at, count)], results[p].at[kind], store_sem.at[kind, p]
                        )
                        for p, (slot, at, count) in enumerate(pieces)
                        if slot == s
                    ]
                    for copy in here:
                        copy.start()
                    stores += here
            else:
                copy = pltpu.make_async_copy(total, results[kind], acc_sem.at[kind])
                copy.start()
                stores.append(copy)
        for copy in stores:
            copy.wait()


def run_adds(scal, accs, after, parts, pieces, *, n_col, width, f_total, last):
    tokens = parts[0][1].shape[3]
    kg = sum(t.shape[0] for t in parts[0][2])
    first = accs is None
    anywhere = pl.BlockSpec(memory_space=pl.ANY)
    per = 2 if all(stash.shape[1] % 2 == 0 and at % 2 == 0 for _, stash, _, at in parts) else 1
    segments, specs, operands, before = [], [], [], 0
    for f_first, stash, tiles, at in parts:
        steps = stash.shape[1] // per

        def spot(f, before=before, steps=steps):
            return jnp.clip(f - before, 0, steps - 1)

        specs.append(pl.BlockSpec((3, per, BS, tokens), lambda f, scal, spot=spot: (0, spot(f), 0, 0)))
        for t in tiles:
            specs.append(
                pl.BlockSpec(
                    (t.shape[0], 3, per, BS, BS),
                    lambda f, scal, spot=spot, start=at // per: (0, 0, spot(f) + start, 0, 0),
                )
            )
        operands += [stash, *tiles]
        segments.append((f_first, at, steps))
        before += steps
    acc_shape = (n_col * width // BS, BS, tokens)
    if last:
        results = [jax.ShapeDtypeStruct((2, count, BS, tokens), BF) for _, _, count in pieces]
    else:
        results = [jax.ShapeDtypeStruct(acc_shape, F32)] * 2
    kernel = functools.partial(
        add_kernel,
        n_col=n_col,
        pieces=pieces,
        groups=len(parts[0][2]),
        waits=len(after),
        segments=segments,
        per=per,
        kg=kg,
        f_total=f_total,
        blocks=width // BS,
        first=first,
        last=last,
    )
    return pl.pallas_call(
        kernel,
        grid_spec=pltpu.PrefetchScalarGridSpec(
            num_scalar_prefetch=1,
            grid=(before,),
            in_specs=[anywhere] * (len(after) + (0 if first else 2)) + specs,
            out_specs=[anywhere] * len(results),
            scratch_shapes=[pltpu.VMEM(acc_shape, F32)] * 2
            + ([pltpu.VMEM(acc_shape, BF)] * 2 if last else [])
            + [pltpu.SemaphoreType.DMA((2,)), pltpu.SemaphoreType.DMA((2, len(pieces)))],
        ),
        out_shape=results,
        compiler_params=pltpu.CompilerParams(vmem_limit_bytes=56 * 1024 * 1024),
        cost_estimate=pl.CostEstimate(
            flops=3 * 2 * tokens * before * per * kg * BS * BS, bytes_accessed=48 * 1024 * 1024, transcendentals=0
        ),
        name="ffn_adds",
    )(scal, *after, *([] if first else accs), *operands)


def total_of(*terms):
    value = terms[0].astype(F32)
    for term in terms[1:]:
        value = value + term.astype(F32)
    return value.astype(BF)


def make_shards(n_row, n_col):
    nz = n_row // 2
    across = [(r, r ^ 1) for r in range(n_row)]
    two_phase = n_col == 4

    def right(first, stop):
        return [(2 * z + c, 2 * z + 2 + c) for z in range(first, stop) for c in (0, 1)]

    def left(first, stop):
        return [(2 * z + c, 2 * z - 2 + c) for z in range(first, stop) for c in (0, 1)]

    def over(value, offset):
        return lax.ppermute(value, "col", [(i, i ^ offset) for i in range(n_col)])

    def swap(value):
        return lax.ppermute(value, "row", across)

    def pieces_of(blocks):
        half = blocks // 2
        if two_phase:
            return ((0, 0, blocks), (1, 0, blocks), (2, 0, blocks), (3, 0, half), (3, half, blocks - half))
        return tuple((s, 0, blocks) for s in range(n_col))

    def sum_columns(parts):
        if two_phase:
            mine, beside, above, low, high = parts
            half = low.shape[1]
            low, high = over(low, 1), over(high, 2)
            above = jnp.concatenate([total_of(above[:, :half], low), above[:, half:]], axis=1)
            beside = jnp.concatenate([beside[:, :half], total_of(beside[:, half:], high)], axis=1)
            got = [over(beside, 1), over(above, 2)]
        else:
            mine = parts[0]
            got = [over(parts[o], o) for o in range(1, n_col)]
        sums = [total_of(mine[i], *[g[i] for g in got]) for i in range(2)]
        return [total.reshape(-1, total.shape[-1]).T for total in sums]

    class Chain:
        def __init__(self, z, own=None, grads=None):
            self.z, self.own, self.grads = z, own, grads
            self.from_left, self.from_right = [], []
            self.tick = 0 if own is not None else 1

        def part(self, slot):
            return [g[slot // 2] for g in self.grads[slot % 2 :: 2]]

        def run(self, count):
            for _ in range(count):
                i = self.tick
                summing = self.grads is not None
                if i == 0:
                    to_right = to_left = self.own
                elif not summing:
                    to_right, to_left = self.from_left[-1], self.from_right[-1]
                else:
                    to_right = total_of(*self.part(i), *self.from_left[-1:])
                    to_left = total_of(*self.part(nz - i), *self.from_right[-1:])
                    if self.own is not None:
                        to_right = jnp.where(self.z >= i, self.from_left[-1], to_right)
                        to_left = jnp.where(nz - 1 - self.z >= i, self.from_right[-1], to_left)
                start = 0 if summing else i
                stop = nz - 1 if self.own is not None else i
                self.from_left.append(lax.ppermute(to_right, "row", right(start, stop)))
                self.from_right.append(lax.ppermute(to_left, "row", left(nz - stop, nz - start)))
                self.tick += 1
            return self

        def received(self, i):
            return (self.from_left[i], self.from_right[i])

        def tie(self, i, other):
            self.from_left[i], self.from_right[i], _ = lax.optimization_barrier((*self.received(i), other))

        def slots(self):
            found = [self.own]
            for o in range(1, nz):
                found.append(jnp.where(self.z >= o, self.from_left[o - 1], self.from_right[nz - o - 1]))
            return found

        def total(self):
            return total_of(*self.part(0), self.from_left[-1], self.from_right[-1])

    class Halves:
        def __init__(self, z, grads):
            self.even_z = z % 2 == 0
            self.grads = grads
            self.near = lax.ppermute(total_of(grads[1], grads[3]), "row", [(r, r ^ 2) for r in range(n_row)])

        def finish(self, after=()):
            keep, _, got, _ = self.grads
            near, _ = lax.optimization_barrier((self.near, after))
            far = jnp.where(self.even_z, near[1], near[0])
            self.mine = jnp.where(self.even_z, near[0], near[1])
            self.rest = lax.ppermute(total_of(keep[1], got[1], far), "row", [(r, r ^ 4) for r in range(n_row)])
            return self

        def total(self):
            keep, _, got, _ = self.grads
            return total_of(keep[0], got[0], self.mine, self.rest)

    def shards(tokens, out_grad, gate_weight, up_weight, down_weight, gate_rows, up_rows, down_columns):
        f_total, part = gate_weight.shape[:2]
        kg = gate_rows.shape[1]
        row = lax.axis_index("row")
        z, core = row // 2, row % 2
        whole_tiles = part == BS
        slots = list(range(0, nz, 2)) + list(range(1, nz, 2))
        spots = (z - jnp.array(slots, dtype=jnp.int32)) % nz
        order = jnp.concatenate([2 * spots + core, 2 * spots + 1 - core]) if whole_tiles else spots
        scal = jnp.concatenate(
            [t.reshape(-1) for t in (gate_rows, up_rows, down_columns)]
            + [order.astype(jnp.int32), lax.axis_index("col").astype(jnp.int32).reshape(1)]
        )
        pieces = pieces_of(tokens.shape[1] // BS)
        panels = lax.all_gather(jnp.stack([tokens, out_grad]), "col")

        def own_tiles(start, stop):
            return jnp.stack([w[start:stop] for w in (gate_weight, up_weight, down_weight)])

        def all_tiles(mine):
            even, odd = jnp.stack(mine[0::2]), jnp.stack(mine[1::2])
            other_even, other_odd = swap(even), swap(odd)
            if whole_tiles:
                return [even, odd, other_even, other_odd]
            return [
                jnp.where(core == 0, jnp.concatenate([a, b], -2), jnp.concatenate([b, a], -2))
                for a, b in ((even, other_even), (odd, other_odd))
            ]

        def exchanged(tile_grads, hold):
            if whole_tiles:
                keep, give = tile_grads[:2], tile_grads[2:]
            else:
                keep = [lax.dynamic_slice_in_dim(g, core * part, part, 4) for g in tile_grads]
                give = [lax.dynamic_slice_in_dim(g, (1 - core) * part, part, 4) for g in tile_grads]
            give, _ = lax.optimization_barrier((give, hold))
            got_odd = swap(give[1])
            return [keep[0], keep[1], swap(give[0]), got_odd]

        width = tokens.shape[1]

        def compute(f_first, f_here, tiles, tile_first, after=(), hold=()):
            tile_grads, stash = run_grads(
                scal, panels, after, tiles, f_total=f_total, f_first=f_first, f_here=f_here, tile_first=tile_first
            )
            return exchanged(tile_grads, hold), (f_first, stash, tiles, tile_first)

        def add_up(accs, parts, last, after=()):
            return run_adds(scal, accs, after, parts, pieces, n_col=n_col, width=width, f_total=f_total, last=last)

        if f_total % 7 == 0 and f_total > 7 and nz == 4 and whole_tiles:
            few = f_total // 7
            at = [0, few, 3 * few, 4 * few, 6 * few, 7 * few]
            tiles = all_tiles(Chain(z, own_tiles(at[0], at[2])).run(3).slots())
            one, two, three = [Chain(z, own_tiles(at[i], at[i + 1])) for i in (2, 3, 4)]
            one.run(1)
            two.run(1)
            one.grads, part_0 = compute(at[0], few, tiles, at[0], (), one.received(0))
            one.run(1)
            two.grads, part_1 = compute(
                at[1], 2 * few, tiles, at[1], (one.grads[3],), one.received(1) + two.received(0)
            )
            one.tie(1, two.grads[0])
            accs = add_up(None, [part_0, part_1], False)
            one.run(1)
            two.run(1)
            one.tie(2, accs[0])
            mine = one.slots()
            one.run(1)
            two.run(1)
            three.run(1)
            three.grads, part_2 = compute(
                at[2], few, all_tiles(mine), 0, (), three.received(0) + two.received(1)
            )
            three.run(1)
            grads, part_3 = compute(
                at[3], 2 * few, all_tiles(two.slots()), 0, (three.grads[3],), three.received(1) + one.received(3)
            )
            fourth = Halves(z, grads)
            three.run(1)
            mine = three.slots()
            last, part_4 = compute(at[4], few, all_tiles(mine), 0, (grads[3],))
            accs = add_up(accs, [part_2, part_3, part_4], True, (last[3],))
            *accs, _ = lax.optimization_barrier((*accs, fourth.near))
            two.run(1)
            fifth = Halves(z, last)
            fourth.finish()
            three.tie(2, fifth.near)
            three.run(1)
            fifth.finish((fourth.rest,))
            sums = [one.total(), two.total(), three.total(), fourth.total(), fifth.total()]
        else:
            gather = Chain(z, own_tiles(0, f_total)).run(nz - 1)
            grads, part_0 = compute(0, f_total, all_tiles(gather.slots()), 0)
            accs = add_up(None, [part_0], True)
            sums = [Chain(z, None, grads).run(nz - 1).total()]

        output, input_grad = sum_columns(accs)
        weight_grads = [jnp.concatenate([jnp.swapaxes(g[kind], 1, 2) for g in sums], axis=0) for kind in range(3)]
        return (output, input_grad, *weight_grads)

    return shards


def solution(mesh):
    in_specs = (
        P("row", "col"),
        P("row", "col"),
        P("col", "row", None),
        P("col", "row", None),
        P("col", "row", None),
        P("col", None),
        P("col", None),
        P("col", None),
    )
    out_specs = in_specs[:5]
    shards = make_shards(mesh.shape["row"], mesh.shape["col"])
    return jax.shard_map(shards, mesh=mesh, in_specs=in_specs, out_specs=out_specs, check_vma=False)
```
